512 devices in a mesh: segment: 32 (over y, x, core), tensor: 16 (over z).
Axes of the slice: x: 4, y: 4, z: 16, core: 2. Of those that a mesh axis runs over, the one named last changes fastest.
Arguments:
- h_init: bfloat16 [256, 4096], P('segment', 'tensor'), may hold values from -6 to 6
- y_init: bfloat16 [256, 4096], P('segment', 'tensor'), may hold values from -6 to 6
- norm_gain: bfloat16 [32, 4096], P('segment'), may hold values from 0.099609375 to 1.8984375
- w_query: bfloat16 [32, 4096, 4096], P('segment', None, 'tensor'), may hold values from -0.09375 to 0.09375
- w_kv: bfloat16 [32, 4096, 1024], P('segment', 'tensor'), may hold values from -0.09375 to 0.09375
- w_out: bfloat16 [32, 4096, 4096], P('segment', 'tensor'), may hold values from -0.09375 to 0.09375
- cache: bfloat16 [32, 16, 224, 1024], P('segment', None, 'tensor'), may hold values from -400 to 400
- lengths: int32 [256], replicated, may hold values from 1 to 224, as said below
Outputs:
- h_final: bfloat16 [256, 4096], P('segment', 'tensor')
- y_final: bfloat16 [256, 4096], P('segment', 'tensor')
The draws below stay inside these ranges and needn't reach their ends.
Inputs may be any that keep to these rules, and one draw needn't show every extreme that they name: `lengths`: some row has exactly 224 cached positions.
All inputs are finite; a program needn't handle non-finite values.
Results may differ from the reference program's by a relative error of at most 0.025.
The reference program's roundings to bfloat16 on the way count: a program that leaves them out, or rounds other values in their place, can miss the bound.
Values may be sent and summed in bfloat16 or wider, within the bound.
A program may use at most 64 MiB of HBM per device.

```python
import jax
import jax.numpy as jnp
from jax import lax

D = 4096
HEADS = 32
KVH = 4
HD = 128
CACHE = 224
MB = 8
TICKS = 2
SEGMENTS = 32
ROWS = 256


def draw_cache(key, part):
    key = jax.random.fold_in(key, 11)
    base_key = jax.random.fold_in(key, 0)
    shape = (SEGMENTS, TICKS * MB, CACHE, 2 * KVH * HD)
    values = jax.random.normal(base_key, shape, jnp.float32)
    return values.astype(jnp.bfloat16)


def draw_lengths(key, part):
    key = jax.random.fold_in(key, 7)
    drawn = jax.random.randint(key, (SEGMENTS * MB,), 1, CACHE + 1)
    return drawn.at[0].set(CACHE).astype(jnp.int32)


def shard_levels(rng, shape, cuts, low, high):
    gain, own = 1.0, jax.random.fold_in(rng, 6)
    for dim, shards_of in cuts:
        draws = jnp.exp(jax.random.uniform(jax.random.fold_in(own, dim), (shards_of,), jnp.float32, low / len(cuts), high / len(cuts)))
        gain = gain * jnp.repeat(draws, shape[dim] // shards_of).reshape([-1 if axis == dim else 1 for axis in range(len(shape))])
    return gain


def normal_values(rng, extent, spread, bound, cuts=(), kind=jnp.bfloat16):
    level = shard_levels(rng, extent, cuts, -0.22, 0.18) if cuts else 1.0
    entries = jax.random.normal(rng, extent, jnp.float32) * spread * level
    return jnp.minimum(jnp.maximum(entries, -bound), bound).astype(kind)


def setup_inputs(seed: int = 0) -> dict:
    streams_of = jax.random.split(jax.random.key(seed), 9)
    h_init = normal_values(streams_of[0], (ROWS, D), 1.0, 6.0, ((0, 32), (1, 16)))
    y_init = normal_values(streams_of[1], (ROWS, D), 1.0, 6.0, ((0, 32), (1, 16)))
    norm_gain = jnp.clip(1.0 + 0.18 * jax.random.normal(streams_of[2], (SEGMENTS, D), jnp.float32), 0.099609375, 1.8984375).astype(jnp.bfloat16)
    w_query = normal_values(streams_of[3], (SEGMENTS, D, HEADS * HD), D ** -0.5, 0.09375, ((0, 32), (2, 16)))
    w_kv = normal_values(streams_of[4], (SEGMENTS, D, 2 * KVH * HD), D ** -0.5, 0.09375, ((0, 32), (1, 16)))
    w_out = normal_values(streams_of[5], (SEGMENTS, HEADS * HD, D), (HEADS * HD) ** -0.5, 0.09375, ((0, 32), (1, 16)))
    cache = draw_cache(jax.random.fold_in(streams_of[8], 71), 0)
    lengths = draw_lengths(jax.random.fold_in(streams_of[8], 71), 0)
    return dict(h_init=h_init, y_init=y_init, norm_gain=norm_gain, w_query=w_query, w_kv=w_kv, w_out=w_out, cache=cache, lengths=lengths)


theta_base = 500000.0
eps_norm = 1e-05
masked_score = -1e+30

def rotate(values, positions):
    row_count = values.shape[0]
    head_count = values.shape[1] // HD
    half_size = HD // 2
    freqs = jnp.exp(-jnp.log(theta_base) * (2.0 * jnp.arange(half_size, dtype=jnp.float32) / HD))
    angles = positions.astype(jnp.float32)[:, None] * freqs[None, :]
    cosine = jnp.cos(angles)[:, None, :]
    sine = jnp.sin(angles)[:, None, :]
    shaped = values.reshape(row_count, head_count, HD)
    first_half = shaped[..., :half_size]
    second_half = shaped[..., half_size:]
    turned = jnp.concatenate([first_half * cosine - second_half * sine, second_half * cosine + first_half * sine], axis=-1)
    return turned.reshape(row_count, head_count * HD)

def section_block(operands):
    state, waiting, seen, gain_row, query_weight, kv_weight, out_weight, cache_rows = operands
    widened = state.astype(jnp.float32)
    normed = (widened * lax.rsqrt(lax.optimization_barrier(jnp.mean(widened * widened, axis=-1, keepdims=True)) + eps_norm) * gain_row.astype(jnp.float32)).astype(jnp.bfloat16)
    queries = rotate(jnp.dot(normed, query_weight, preferred_element_type=jnp.float32), seen).astype(jnp.bfloat16)
    key_width = KVH * HD
    fresh = jnp.dot(normed, kv_weight, preferred_element_type=jnp.float32)
    fresh = jnp.concatenate([rotate(fresh[:, :key_width], seen), fresh[:, key_width:]], axis=1).astype(jnp.bfloat16)
    group_size = HEADS // KVH
    row_count = state.shape[0]
    softmax_scale = HD ** (-0.5)
    query_head_rows = queries.astype(jnp.float32).reshape(row_count, KVH, group_size, HD)
    cached_keys = cache_rows[..., :key_width].astype(jnp.float32).reshape(row_count, CACHE, KVH, HD)
    cached_values = cache_rows[..., key_width:].astype(jnp.float32).reshape(row_count, CACHE, KVH, HD)
    incoming_keys = fresh[:, :key_width].astype(jnp.float32).reshape(row_count, KVH, HD)
    incoming_values = fresh[:, key_width:].astype(jnp.float32).reshape(row_count, KVH, HD)
    scores = jnp.einsum('bkgd,bpkd->bkgp', query_head_rows, cached_keys) * softmax_scale
    valid = jnp.arange(CACHE, dtype=jnp.int32)[None, :] < seen[:, None]
    scores = jnp.where(valid[:, None, None, :], scores, masked_score)
    self_token_score = jnp.einsum('nfcz,nfz->nfc', query_head_rows, incoming_keys) * softmax_scale
    peak = jnp.maximum(lax.optimization_barrier(jnp.max(scores, axis=-1)), self_token_score)
    weights = jnp.where(valid[:, None, None, :], jnp.exp(scores - peak[..., None]), 0.0)
    own_weight = jnp.exp(self_token_score - peak)
    denominator = lax.optimization_barrier(jnp.sum(weights, axis=-1)) + own_weight
    mixed = jnp.einsum('bkgp,bpkd->bkgd', weights, cached_values) + own_weight[..., None] * incoming_values[:, :, None, :]
    attended_context = (mixed / denominator[..., None]).reshape(row_count, HEADS * HD).astype(jnp.bfloat16)
    block_out = jnp.dot(attended_context, out_weight, preferred_element_type=jnp.float32).astype(jnp.bfloat16)
    advanced = (widened + waiting.astype(jnp.float32)).astype(jnp.bfloat16)
    return (advanced, block_out)

def reference(h_init, y_init, norm_gain, w_query, w_kv, w_out, cache, lengths):
    state = h_init.reshape(SEGMENTS, MB, D)
    waiting = y_init.reshape(SEGMENTS, MB, D)
    by_batch = lengths.reshape(SEGMENTS, MB)
    advanced = state
    block_out = waiting
    for step_index in range(TICKS):
        batch_index = jnp.arange(SEGMENTS, dtype=jnp.int32) - step_index
        picked = by_batch[jnp.maximum(batch_index, 0)]
        seen = jnp.where(batch_index[:, None] >= 0, picked, 0).astype(jnp.int32)
        rows_now = cache[:, step_index * MB:(step_index + 1) * MB]
        advanced, block_out = lax.map(section_block, (state, waiting, seen, norm_gain, w_query, w_kv, w_out, rows_now))
        if step_index + 1 < TICKS:
            state = jnp.concatenate([jnp.zeros_like(advanced[:1]), advanced[:-1]], axis=0)
            waiting = jnp.concatenate([jnp.zeros_like(block_out[:1]), block_out[:-1]], axis=0)
    return (advanced.reshape(SEGMENTS * MB, D), block_out.reshape(SEGMENTS * MB, D))
```

```python
import functools
import math

import jax
import jax.numpy as jnp
from jax import lax
from jax.experimental import pallas as pl
from jax.experimental.pallas import tpu as pltpu
from jax.sharding import PartitionSpec as P

HEADS = 32
KVH = 4
HD = 128
TICKS = 2
MB = 8
ROWS2 = TICKS * MB
THETA = 500000.0
EPS = 1e-05
MASKED = -1e30
BIG = 1 << 30
MESH = pl.DeviceIdType.MESH
F32 = jnp.float32
BF16 = jnp.bfloat16


def far_first(i, me, n):
    d = n // 2 - (i + 1) // 2
    off = jnp.where(lax.rem(i, 2) == 1, d, n - d)
    return lax.rem(me + off, n)


def drain(ref, sem):
    pltpu.make_async_copy(ref, ref, sem).wait()


def stack_halves(v):
    return jnp.concatenate([v[:, :HD], v[:, HD:]], axis=0)


def unstack(v):
    return jnp.concatenate([v[:MB], v[MB:]], axis=1)


def kernel(
    n, n_seg, h_hbm, y_hbm, gain_hbm, wq_hbm, wkv_hbm, wo_hbm, cache_hbm, len_ref,
    hfin_ref, yfin_ref,
    h_in, y_in, gain, wq, wkv, wo, cache,
    hsrc, asrc, hbuf, abuf, nbuf, cosb, sinb,
    qsrc, qbuf, kvsrc, kvbuf, kbuf, vbuf, qt, ot,
    osrc, obuf, ssrc, sbuf,
    d0src, d1src, d0buf, d1buf,
    load_sem, send_sem, recv_sem,
):
    me = lax.axis_index("tensor")
    seg = lax.axis_index("segment")
    first = seg == 0
    last = seg == n_seg - 1
    span = cache_hbm.shape[2]

    barrier = pltpu.get_barrier_semaphore()

    def tell(i, carry):
        pl.semaphore_signal(
            barrier, 1, device_id={"tensor": far_first(i, me, n)}, device_id_type=MESH
        )
        return carry

    lax.fori_loop(0, n - 1, tell, 0)

    @pl.when(seg > 0)
    def _():
        def tell_back(i, carry):
            pl.semaphore_signal(
                barrier, 1, device_id={"segment": seg - 1, "tensor": i}, device_id_type=MESH
            )
            return carry

        lax.fori_loop(0, n, tell_back, 0)

    loads = [
        pltpu.make_async_copy(src, dst, load_sem.at[k])
        for k, (src, dst) in enumerate(
            [
                (h_hbm, h_in), (y_hbm, y_in), (gain_hbm, gain), (cache_hbm, cache),
                (wkv_hbm, wkv), (wq_hbm, wq), (wo_hbm, wo),
            ]
        )
    ]
    for load in loads:
        load.start()
    loads[0].wait()
    loads[1].wait()

    h32 = h_in[...].astype(F32)
    a32 = (h32 + y_in[...].astype(F32)).astype(BF16).astype(F32)
    h_block = stack_halves(h32).astype(BF16)
    hsrc[...] = h_block
    asrc[...] = stack_halves(a32).astype(BF16)
    hbuf[me] = h_block

    row16 = lax.broadcasted_iota(jnp.int32, (ROWS2, HD), 0)
    lane16 = lax.broadcasted_iota(jnp.int32, (ROWS2, HD), 1)
    base1 = jnp.maximum(seg - 1, 0) * MB
    seen = [len_ref[seg * MB + b] for b in range(MB)] + [
        jnp.where(first, 0, len_ref[base1 + b]) for b in range(MB)
    ]
    seen_rows = jnp.zeros((ROWS2, HD), jnp.int32)
    for b in range(ROWS2):
        seen_rows = jnp.where(row16 == b, seen[b], seen_rows)
    half_lane = jnp.where(lane16 < HD // 2, lane16, lane16 - HD // 2)
    freqs = jnp.exp(-math.log(THETA) * (2.0 * half_lane.astype(F32) / HD))
    angles = seen_rows.astype(F32) * freqs
    sines = jnp.sin(angles)
    cosb[...] = jnp.cos(angles)
    sinb[...] = jnp.where(lane16 < HD // 2, -sines, sines)

    pl.semaphore_wait(barrier, jnp.where(last, n - 1, 2 * n - 1))

    def send_state(i, carry):
        peer = far_first(i, me, n)
        pltpu.make_async_remote_copy(
            hsrc, hbuf.at[me], send_sem.at[0], recv_sem.at[0],
            device_id={"tensor": peer}, device_id_type=MESH,
        ).start()
        return carry

    def send_both(i, carry):
        peer = far_first(i, me, n)
        pltpu.make_async_remote_copy(
            asrc, abuf.at[me], send_sem.at[1], recv_sem.at[1],
            device_id={"segment": seg + 1, "tensor": peer}, device_id_type=MESH,
        ).start()
        return send_state(i, carry)

    @pl.when(seg < n_seg - 1)
    def _():
        lax.fori_loop(0, n - 1, send_both, 0)
        pltpu.make_async_remote_copy(
            asrc, abuf.at[me], send_sem.at[1], recv_sem.at[1],
            device_id={"segment": seg + 1, "tensor": me}, device_id_type=MESH,
        ).start()

    @pl.when(last)
    def _():
        lax.fori_loop(0, n - 1, send_state, 0)

    loads[3].wait()
    pad = jnp.zeros((16 - span, HD), F32)
    for b in range(ROWS2):
        rows = cache[0, b].astype(F32)
        for dst, start in ((kbuf, 0), (vbuf, KVH * HD)):
            dst[b] = jnp.concatenate(
                [
                    piece
                    for g in range(KVH)
                    for piece in (rows[:, start + g * HD : start + (g + 1) * HD], pad)
                ],
                axis=0,
            ).astype(BF16)
    loads[2].wait()

    @pl.when(first)
    def _():
        abuf[...] = jnp.zeros_like(abuf)
        d0buf[...] = jnp.zeros_like(d0buf)

    loads[4].wait()
    loads[5].wait()
    drain(hbuf.at[pl.ds(0, n - 1)], recv_sem.at[0])

    @pl.when(seg > 0)
    def _():
        drain(abuf, recv_sem.at[1])

    chunks = []
    for z in range(n):
        hz = hbuf[z].astype(F32)
        az = abuf[z].astype(F32)
        chunks.append(jnp.concatenate([hz[:MB], az[:MB]], axis=0))
        chunks.append(jnp.concatenate([hz[MB:], az[MB:]], axis=0))
    squares = [c * c for c in chunks]
    while len(squares) > 1:
        squares = [a + b for a, b in zip(squares[::2], squares[1::2])]
    mean = jnp.sum(squares[0], axis=-1, keepdims=True) / (n * 2 * HD)
    inv = lax.rsqrt(mean + EPS)
    normed = []
    for k, c in enumerate(chunks):
        g = gain[0:1, k * HD : (k + 1) * HD].astype(F32)
        normed.append((c * inv * g).astype(BF16))
    for z in range(n):
        nbuf[z] = jnp.concatenate(normed[2 * z : 2 * z + 2], axis=1)
    kv = jnp.dot(nbuf[me], wkv[0], preferred_element_type=F32)
    for c in range(2 * KVH):
        kvsrc[pl.ds(c, ROWS2, stride=2 * KVH), :] = kv[:, c * HD : (c + 1) * HD]
    q32 = jnp.dot(jnp.concatenate(normed, axis=1), wq[0], preferred_element_type=F32)
    cosine = cosb[...]
    sine = sinb[...]
    turned = []
    for i in range(2):
        v = q32[:, i * HD : (i + 1) * HD]
        turned.append(v * cosine + pltpu.roll(v, HD // 2, 1) * sine)
    q = jnp.concatenate(turned, axis=1).astype(BF16)
    qsrc[...] = q
    qbuf[me] = q
    kvbuf[me] = kvsrc[pl.ds(pl.multiple_of(me * 8, 8), 8), :]

    def send_query(i, carry):
        peer = far_first(i, me, n)
        pltpu.make_async_remote_copy(
            kvsrc.at[pl.ds(pl.multiple_of(peer * 8, 8), 8)], kvbuf.at[me],
            send_sem.at[3], recv_sem.at[3],
            device_id={"tensor": peer}, device_id_type=MESH,
        ).start()
        pltpu.make_async_remote_copy(
            qsrc, qbuf.at[me], send_sem.at[2], recv_sem.at[2],
            device_id={"tensor": peer}, device_id_type=MESH,
        ).start()
        return carry

    lax.fori_loop(0, n - 1, send_query, 0)

    jrow = lax.broadcasted_iota(jnp.int32, (HEADS, KVH * 16), 0)
    kcol = lax.broadcasted_iota(jnp.int32, (HEADS, KVH * 16), 1)
    same = lax.rem(jrow, 16) // 4 == kcol // 16
    slot = lax.rem(kcol, 16)
    place = jnp.where(same & (slot < span), me * span + slot, BIG)
    own_slot = same & (slot == span)
    lane32 = lax.broadcasted_iota(jnp.int32, (HEADS, HD), 1)

    drain(kvbuf.at[pl.ds(0, n - 1)], recv_sem.at[3])
    fresh = kvbuf[0]
    for z in range(1, n):
        fresh = fresh + kvbuf[z]
    fresh_k = fresh[:KVH]
    fresh_k = (
        fresh_k * cosb[pl.ds(me, 1), :]
        + pltpu.roll(fresh, HD // 2, 1)[:KVH] * sinb[pl.ds(me, 1), :]
    )
    fresh_v = fresh[KVH:]
    krow = lax.broadcasted_iota(jnp.int32, (KVH * 16, HD), 0)
    for dst, val in ((kbuf, fresh_k), (vbuf, fresh_v)):
        spread = jnp.concatenate(
            [jnp.broadcast_to(val[g : g + 1], (16, HD)) for g in range(KVH)], axis=0
        )
        dst[me] = jnp.where(lax.rem(krow, 16) == span, spread, dst[me].astype(F32)).astype(BF16)

    drain(qbuf.at[pl.ds(0, n - 1)], recv_sem.at[2])
    for r in range(n):
        v = qbuf[r].astype(F32)
        qt[0, pl.ds(r, ROWS2, stride=n), :] = v[:, :HD]
        qt[1, pl.ds(r, ROWS2, stride=n), :] = v[:, HD:]

    stats = jnp.zeros((HEADS, HD), F32)
    scale = HD ** (-0.5)
    for b in range(ROWS2):
        qb = jnp.concatenate(
            [qt[0, b * n : (b + 1) * n, :], qt[1, b * n : (b + 1) * n, :]], axis=0
        ).astype(BF16)
        s = (
            lax.dot_general(
                qb, kbuf[b], (((1,), (1,)), ((), ())), preferred_element_type=F32
            )
            * scale
        )
        own_place = jnp.where(me == b, -1, BIG)
        valid = jnp.where(own_slot, own_place, place) < seen[b]
        s = jnp.where(valid, s, MASKED)
        peak = jnp.max(s, axis=-1, keepdims=True)
        w = jnp.where(valid, jnp.exp(s - peak), 0.0)
        total = jnp.sum(w, axis=-1, keepdims=True)
        mixed = jnp.dot(w.astype(BF16), vbuf[b], preferred_element_type=F32)
        ot[0, b * n : (b + 1) * n, :] = mixed[:n]
        ot[1, b * n : (b + 1) * n, :] = mixed[n:]
        stats = jnp.where(lane32 == b, peak, stats)
        stats = jnp.where(lane32 == ROWS2 + b, total, stats)
    packed = jnp.where(lane32[:n] < 2 * ROWS2, stats[:n], pltpu.roll(stats[n:], 2 * ROWS2, 1))
    for r in range(n):
        ssrc[r] = packed[r : r + 1, :]
        osrc[r] = jnp.concatenate(
            [ot[0, pl.ds(r, ROWS2, stride=n), :], ot[1, pl.ds(r, ROWS2, stride=n), :]], axis=1
        ).astype(BF16)
    obuf[me] = osrc[me]
    sbuf[me] = ssrc[me]

    def send_partial(i, carry):
        peer = far_first(i, me, n)
        pltpu.make_async_remote_copy(
            ssrc.at[peer], sbuf.at[me], send_sem.at[5], recv_sem.at[5],
            device_id={"tensor": peer}, device_id_type=MESH,
        ).start()
        pltpu.make_async_remote_copy(
            osrc.at[peer], obuf.at[me], send_sem.at[4], recv_sem.at[4],
            device_id={"tensor": peer}, device_id_type=MESH,
        ).start()
        return carry

    lax.fori_loop(0, n - 1, send_partial, 0)
    drain(sbuf.at[pl.ds(0, n - 1)], recv_sem.at[5])
    by_row = jnp.transpose(jnp.concatenate([sbuf[r] for r in range(n)], axis=0))
    shares = []
    for i in range(2):
        peaks = by_row[i * 32 : i * 32 + 16]
        totals = by_row[i * 32 + 16 : i * 32 + 32]
        scales = jnp.exp(peaks - jnp.max(peaks, axis=-1, keepdims=True))
        shares.append(scales / jnp.sum(scales * totals, axis=-1, keepdims=True))
    loads[6].wait()
    drain(obuf.at[pl.ds(0, n - 1)], recv_sem.at[4])
    context = [jnp.zeros((ROWS2, HD), F32), jnp.zeros((ROWS2, HD), F32)]
    for r in range(n):
        v = obuf[r].astype(F32)
        for i in range(2):
            context[i] = context[i] + v[:, i * HD : (i + 1) * HD] * shares[i][:, r : r + 1]
    ctx = jnp.concatenate(context, axis=1).astype(BF16)

    out = jnp.dot(ctx, wo[0], preferred_element_type=F32)
    for c in range(n):
        block = out[:, c * 256 : (c + 1) * 256]
        d0src[c] = stack_halves(block[:MB]).astype(BF16)
        d1src[c] = stack_halves(block[MB:]).astype(BF16)
    d1buf[me] = d1src[me]

    def send_out(i, carry):
        peer = far_first(i, me, n)
        pltpu.make_async_remote_copy(
            d1src.at[peer], d1buf.at[me], send_sem.at[7], recv_sem.at[7],
            device_id={"tensor": peer}, device_id_type=MESH,
        ).start()
        return carry

    def send_outs(i, carry):
        peer = far_first(i, me, n)
        pltpu.make_async_remote_copy(
            d0src.at[peer], d0buf.at[me], send_sem.at[6], recv_sem.at[6],
            device_id={"segment": seg + 1, "tensor": peer}, device_id_type=MESH,
        ).start()
        return send_out(i, carry)

    @pl.when(seg < n_seg - 1)
    def _():
        lax.fori_loop(0, n - 1, send_outs, 0)
        pltpu.make_async_remote_copy(
            d0src.at[me], d0buf.at[me], send_sem.at[6], recv_sem.at[6],
            device_id={"segment": seg + 1, "tensor": me}, device_id_type=MESH,
        ).start()

    @pl.when(last)
    def _():
        lax.fori_loop(0, n - 1, send_out, 0)

    for _ in range(1):
        pltpu.make_async_copy(hbuf.at[pl.ds(0, n - 1)], hbuf.at[pl.ds(0, n - 1)], send_sem.at[0]).wait()
    drain(qbuf.at[pl.ds(0, n - 1)], send_sem.at[2])
    drain(kvbuf.at[pl.ds(0, n - 1)], send_sem.at[3])
    drain(obuf.at[pl.ds(0, n - 1)], send_sem.at[4])
    drain(sbuf.at[pl.ds(0, n - 1)], send_sem.at[5])

    @pl.when(seg < n_seg - 1)
    def _():
        drain(abuf, send_sem.at[1])

    drain(d1buf.at[pl.ds(0, n - 1)], recv_sem.at[7])

    @pl.when(seg > 0)
    def _():
        drain(d0buf, recv_sem.at[6])

    sums = []
    for buf in (d0buf, d1buf):
        terms = [buf[z].astype(F32) for z in range(n)]
        while len(terms) > 1:
            terms = [a + b for a, b in zip(terms[::2], terms[1::2])]
        sums.append(terms[0].astype(BF16))
    hfin_ref[...] = unstack(abuf[me].astype(F32) + sums[0].astype(F32)).astype(BF16)
    yfin_ref[...] = unstack(sums[1].astype(F32)).astype(BF16)

    drain(d1buf.at[pl.ds(0, n - 1)], send_sem.at[7])

    @pl.when(seg < n_seg - 1)
    def _():
        drain(d0buf, send_sem.at[6])


def solution(mesh):
    n = mesh.shape["tensor"]
    n_seg = mesh.shape["segment"]

    def local(h_init, y_init, norm_gain, w_query, w_kv, w_out, cache, lengths):
        hbm = pl.BlockSpec(memory_space=pl.ANY)
        vmem = pl.BlockSpec(memory_space=pltpu.VMEM)
        smem = pl.BlockSpec(memory_space=pltpu.SMEM)
        tile = (ROWS2, HD)
        wide = (ROWS2, 2 * HD)
        return pl.pallas_call(
            functools.partial(kernel, n, n_seg),
            out_shape=(
                jax.ShapeDtypeStruct(h_init.shape, BF16),
                jax.ShapeDtypeStruct(h_init.shape, BF16),
            ),
            in_specs=[hbm] * 7 + [smem],
            out_specs=(vmem, vmem),
            scratch_shapes=[
                pltpu.VMEM(h_init.shape, BF16),
                pltpu.VMEM(y_init.shape, BF16),
                pltpu.VMEM(norm_gain.shape, BF16),
                pltpu.VMEM(w_query.shape, BF16),
                pltpu.VMEM(w_kv.shape, BF16),
                pltpu.VMEM(w_out.shape, BF16),
                pltpu.VMEM(cache.shape, BF16),
                pltpu.VMEM(tile, BF16),
                pltpu.VMEM(tile, BF16),
                pltpu.VMEM((n,) + tile, BF16),
                pltpu.VMEM((n,) + tile, BF16),
                pltpu.VMEM((n,) + wide, BF16),
                pltpu.VMEM(tile, F32),
                pltpu.VMEM(tile, F32),
                pltpu.VMEM(wide, BF16),
                pltpu.VMEM((n,) + wide, BF16),
                pltpu.VMEM((ROWS2 * 2 * KVH, HD), F32),
                pltpu.VMEM((n, 2 * KVH, HD), F32),
                pltpu.VMEM((ROWS2, KVH * 16, HD), BF16),
                pltpu.VMEM((ROWS2, KVH * 16, HD), BF16),
                pltpu.VMEM((2, ROWS2 * n, HD), F32),
                pltpu.VMEM((2, ROWS2 * n, HD), F32),
                pltpu.VMEM((n,) + wide, BF16),
                pltpu.VMEM((n,) + wide, BF16),
                pltpu.VMEM((n, 1, HD), F32),
                pltpu.VMEM((n, 1, HD), F32),
                pltpu.VMEM((n,) + tile, BF16),
                pltpu.VMEM((n,) + tile, BF16),
                pltpu.VMEM((n,) + tile, BF16),
                pltpu.VMEM((n,) + tile, BF16),
                pltpu.SemaphoreType.DMA((7,)),
                pltpu.SemaphoreType.DMA((8,)),
                pltpu.SemaphoreType.DMA((8,)),
            ],
            compiler_params=pltpu.CompilerParams(
                collective_id=0, has_side_effects=True, vmem_limit_bytes=48 << 20
            ),
        )(h_init, y_init, norm_gain, w_query, w_kv, w_out, cache, lengths)

    return jax.shard_map(
        local,
        mesh=mesh,
        in_specs=(
            P("segment", "tensor"),
            P("segment", "tensor"),
            P("segment", None),
            P("segment", None, "tensor"),
            P("segment", "tensor", None),
            P("segment", "tensor", None),
            P("segment", None, "tensor", None),
            P(),
        ),
        out_specs=(P("segment", "tensor"), P("segment", "tensor")),
        check_vma=False,
    )
```

```python
import functools
import math

import jax
import jax.numpy as jnp
from jax import lax
from jax.experimental import pallas as pl
from jax.experimental.pallas import tpu as pltpu
from jax.sharding import PartitionSpec as P

HEADS = 32
KVH = 4
HD = 128
TICKS = 2
MB = 8
ROWS2 = TICKS * MB
THETA = 500000.0
EPS = 1e-05
MASKED = -1e30
BIG = 1 << 30
MESH = pl.DeviceIdType.MESH
F32 = jnp.float32
BF16 = jnp.bfloat16


def far_first(i, me, n):
    d = n // 2 - (i + 1) // 2
    off = jnp.where(lax.rem(i, 2) == 1, d, n - d)
    return lax.rem(me + off, n)


def drain(ref, sem):
    pltpu.make_async_copy(ref, ref, sem).wait()


def stack_halves(v):
    return jnp.concatenate([v[:, :HD], v[:, HD:]], axis=0)


def unstack(v):
    return jnp.concatenate([v[:MB], v[MB:]], axis=1)


def kernel(
    n, n_seg, h_hbm, y_hbm, gain_hbm, wq_hbm, wkv_hbm, wo_hbm, cache_hbm, len_ref,
    hfin_ref, yfin_ref,
    h_in, y_in, gain, wq, wkv, wo, cache,
    ssrc_state, state, nbuf, cosb, sinb,
    qsrc, qbuf, kvt32, kvsrc, kvbuf, kvt, kbuf, vbuf, qt, ot,
    osrc, obuf, stsrc, stbuf, dsrc, dbuf,
    load_sem, send_sem, recv_sem,
):
    me = lax.axis_index("tensor")
    seg = lax.axis_index("segment")
    first = seg == 0
    not_last = seg < n_seg - 1
    span = cache_hbm.shape[1]
    slots = KVH * 16
    others = pl.ds(0, n - 1)

    barrier = pltpu.get_barrier_semaphore()

    def tell(i, carry):
        pl.semaphore_signal(
            barrier, 1, device_id={"tensor": far_first(i, me, n)}, device_id_type=MESH
        )
        return carry

    lax.fori_loop(0, n - 1, tell, 0)

    @pl.when(seg > 0)
    def _():
        def tell_back(i, carry):
            pl.semaphore_signal(
                barrier, 1, device_id={"segment": seg - 1, "tensor": i}, device_id_type=MESH
            )
            return carry

        lax.fori_loop(0, n, tell_back, 0)

    loads = [
        pltpu.make_async_copy(src, dst, load_sem.at[k])
        for k, (src, dst) in enumerate(
            [
                (h_hbm, h_in), (y_hbm, y_in), (gain_hbm, gain), (cache_hbm, cache),
                (wkv_hbm, wkv), (wq_hbm, wq), (wo_hbm, wo),
            ]
        )
    ]
    for load in loads:
        load.start()
    loads[0].wait()
    loads[1].wait()

    def send_peers(src_of, dst, sems):
        def step(i, carry):
            peer = far_first(i, me, n)
            pltpu.make_async_remote_copy(
                src_of(peer), dst, send_sem.at[sems], recv_sem.at[sems],
                device_id={"tensor": peer}, device_id_type=MESH,
            ).start()
            return carry

        lax.fori_loop(0, n - 1, step, 0)

    def send_next(src_of, dst, sems):
        @pl.when(not_last)
        def _():
            def step(i, carry):
                peer = far_first(i, me, n)
                pltpu.make_async_remote_copy(
                    src_of(peer), dst, send_sem.at[sems], recv_sem.at[sems],
                    device_id={"segment": seg + 1, "tensor": peer}, device_id_type=MESH,
                ).start()
                return carry

            lax.fori_loop(0, n - 1, step, 0)
            pltpu.make_async_remote_copy(
                src_of(me), dst, send_sem.at[sems], recv_sem.at[sems],
                device_id={"segment": seg + 1, "tensor": me}, device_id_type=MESH,
            ).start()

    h32 = h_in[...].astype(F32)
    a32 = (h32 + y_in[...].astype(F32)).astype(BF16).astype(F32)
    h_block = stack_halves(h32).astype(BF16)
    ssrc_state[0] = h_block
    ssrc_state[1] = stack_halves(a32).astype(BF16)
    state[0, me] = h_block

    row16 = lax.broadcasted_iota(jnp.int32, (ROWS2, HD), 0)
    lane16 = lax.broadcasted_iota(jnp.int32, (ROWS2, HD), 1)
    base1 = jnp.maximum(seg - 1, 0) * MB
    seen = [len_ref[seg * MB + b] for b in range(MB)] + [
        jnp.where(first, 0, len_ref[base1 + b]) for b in range(MB)
    ]
    seen_rows = jnp.zeros((ROWS2, HD), jnp.int32)
    for b in range(ROWS2):
        seen_rows = jnp.where(row16 == b, seen[b], seen_rows)
    half_lane = jnp.where(lane16 < HD // 2, lane16, lane16 - HD // 2)
    freqs = jnp.exp(-math.log(THETA) * (2.0 * half_lane.astype(F32) / HD))
    angles = seen_rows.astype(F32) * freqs
    sines = jnp.sin(angles)
    cosb[...] = jnp.cos(angles)
    sinb[...] = jnp.where(lane16 < HD // 2, -sines, sines)

    pl.semaphore_wait(barrier, jnp.where(not_last, 2 * n - 1, n - 1))

    send_peers(lambda peer: ssrc_state.at[0], state.at[0, me], 0)
    send_next(lambda peer: ssrc_state.at[1], state.at[1, me], 1)

    loads[3].wait()
    for p in range(16):
        for g in range(KVH):
            for part in range(2):
                if p < span:
                    col = (part * KVH + g) * HD
                    v = cache[0, p, :, col : col + HD].astype(F32)
                else:
                    v = jnp.zeros((ROWS2, HD), F32)
                kvt[part, pl.ds(g * 16 + p, ROWS2, stride=slots), :] = v
    for b in range(ROWS2):
        for part, dst in enumerate((kbuf, vbuf)):
            dst[b] = kvt[part, b * slots : (b + 1) * slots, :].astype(BF16)
    loads[2].wait()

    @pl.when(first)
    def _():
        state[1] = jnp.zeros_like(state[1])
        dbuf[0] = jnp.zeros_like(dbuf[0])

    loads[4].wait()
    loads[5].wait()
    jrow = lax.broadcasted_iota(jnp.int32, (HEADS, slots), 0)
    kcol = lax.broadcasted_iota(jnp.int32, (HEADS, slots), 1)
    same = lax.rem(jrow, 16) // 4 == kcol // 16
    slot = lax.rem(kcol, 16)
    place = jnp.where(same & (slot < span), me * span + slot, BIG)
    own_slot = same & (slot == span)
    lane32 = lax.broadcasted_iota(jnp.int32, (HEADS, HD), 1)
    krow = lax.broadcasted_iota(jnp.int32, (slots, HD), 0)
    scale = HD ** (-0.5)

    def project(t):
        chunks = []
        for z in range(n):
            v = state[t, z].astype(F32)
            chunks += [v[:MB], v[MB:]]
        squares = [c * c for c in chunks]
        while len(squares) > 1:
            squares = [a + b for a, b in zip(squares[::2], squares[1::2])]
        mean = jnp.sum(squares[0], axis=-1, keepdims=True) / (n * 2 * HD)
        inv = lax.rsqrt(mean + EPS)
        normed = []
        for k, c in enumerate(chunks):
            g = gain[0:1, k * HD : (k + 1) * HD].astype(F32)
            normed.append((c * inv * g).astype(BF16))
        for z in range(n):
            nbuf[z] = jnp.concatenate(normed[2 * z : 2 * z + 2], axis=1)
        kv = jnp.dot(nbuf[me], wkv[0], preferred_element_type=F32)
        for c in range(2 * KVH):
            kvt32[pl.ds(c, MB, stride=2 * KVH), :] = kv[:, c * HD : (c + 1) * HD]
        for o in range(4):
            kvsrc[t, o] = kvt32[o * 16 : (o + 1) * 16, :].astype(BF16)
        q32 = jnp.dot(jnp.concatenate(normed, axis=1), wq[0], preferred_element_type=F32)
        cosine = cosb[t * MB : (t + 1) * MB]
        sine = sinb[t * MB : (t + 1) * MB]
        turned = []
        for i in range(2):
            v = q32[:, i * HD : (i + 1) * HD]
            turned.append(v * cosine + pltpu.roll(v, HD // 2, 1) * sine)
        q = jnp.concatenate(turned, axis=0).astype(BF16)
        qsrc[t] = q
        qbuf[t, me] = q
        for o in range(4):
            owner = 4 * o + 2 * t

            @pl.when(me == owner)
            def _():
                kvbuf[t, owner] = kvsrc[t, o]

            @pl.when(me != owner)
            def _():
                pltpu.make_async_remote_copy(
                    kvsrc.at[t, o], kvbuf.at[t, me], send_sem.at[4 + t], recv_sem.at[4 + t],
                    device_id={"tensor": owner}, device_id_type=MESH,
                ).start()

        send_peers(lambda peer: qsrc.at[t], qbuf.at[t, me], 2 + t)

    def attend(t):
        @pl.when(lax.rem(me, 4) == 2 * t)
        def _():
            drain(kvbuf.at[t, others], recv_sem.at[4 + t])
            terms = [kvbuf[t, z].astype(F32) for z in range(n)]
            while len(terms) > 1:
                terms = [a + b for a, b in zip(terms[::2], terms[1::2])]
            fresh = terms[0]
            rolled = pltpu.roll(fresh, HD // 2, 1)
            for j in range(2):
                row = t * MB + (me // 4) * 2 + j
                at = j * 2 * KVH
                keys = (
                    fresh[at : at + KVH] * cosb[pl.ds(row, 1), :]
                    + rolled[at : at + KVH] * sinb[pl.ds(row, 1), :]
                )
                for dst, val in ((kbuf, keys), (vbuf, fresh[at + KVH : at + 2 * KVH])):
                    spread = jnp.concatenate(
                        [jnp.broadcast_to(val[g : g + 1], (16, HD)) for g in range(KVH)], axis=0
                    )
                    old = dst[row].astype(F32)
                    dst[row] = jnp.where(lax.rem(krow, 16) == span, spread, old).astype(BF16)

        drain(qbuf.at[t, others], recv_sem.at[2 + t])
        for r in range(n):
            v = qbuf[t, r].astype(F32)
            for i in range(2):
                qt[pl.ds(i * n + r, MB, stride=2 * n), :] = v[i * MB : (i + 1) * MB]
        scores = [
            lax.dot_general(
                qt[b * HEADS : (b + 1) * HEADS, :].astype(BF16),
                kbuf[t * MB + b],
                (((1,), (1,)), ((), ())),
                preferred_element_type=F32,
            )
            for b in range(MB)
        ]
        stats = jnp.zeros((HEADS, HD), F32)
        weights = []
        for b in range(MB):
            own_place = jnp.where(me == 4 * (b // 2) + 2 * t, -1, BIG)
            valid = jnp.where(own_slot, own_place, place) < seen[t * MB + b]
            s = jnp.where(valid, scores[b] * scale, MASKED)
            peak = jnp.max(s, axis=-1, keepdims=True)
            w = jnp.where(valid, jnp.exp(s - peak), 0.0)
            total = jnp.sum(w, axis=-1, keepdims=True)
            weights.append(w.astype(BF16))
            stats = jnp.where(lane32 == b, peak, stats)
            stats = jnp.where(lane32 == MB + b, total, stats)
        for b in range(MB):
            ot[b * HEADS : (b + 1) * HEADS, :] = jnp.dot(
                weights[b], vbuf[t * MB + b], preferred_element_type=F32
            )
        packed = jnp.where(lane32[:n] < 2 * MB, stats[:n], pltpu.roll(stats[n:], 2 * MB, 1))
        for r in range(n):
            stsrc[t, r] = packed[r : r + 1, :]
            osrc[t, r] = jnp.concatenate(
                [ot[pl.ds(i * n + r, MB, stride=2 * n), :] for i in range(2)], axis=0
            ).astype(BF16)
        obuf[t, me] = osrc[t, me]
        stbuf[t, me] = stsrc[t, me]
        send_peers(lambda peer: stsrc.at[t, peer], stbuf.at[t, me], 8 + t)
        send_peers(lambda peer: osrc.at[t, peer], obuf.at[t, me], 6 + t)

    def combine(t):
        drain(stbuf.at[t, others], recv_sem.at[8 + t])
        by_row = jnp.transpose(jnp.concatenate([stbuf[t, r] for r in range(n)], axis=0))
        shares = []
        for i in range(2):
            peaks = by_row[i * 16 : i * 16 + 8]
            totals = by_row[i * 16 + 8 : i * 16 + 16]
            scales = jnp.exp(peaks - jnp.max(peaks, axis=-1, keepdims=True))
            shares.append(scales / jnp.sum(scales * totals, axis=-1, keepdims=True))
        share = jnp.concatenate(shares, axis=0)
        drain(obuf.at[t, others], recv_sem.at[6 + t])
        terms = [obuf[t, r].astype(F32) * share[:, r : r + 1] for r in range(n)]
        while len(terms) > 1:
            terms = [a + b for a, b in zip(terms[::2], terms[1::2])]
        ctx = unstack(terms[0]).astype(BF16)
        out = jnp.dot(ctx, wo[0], preferred_element_type=F32)
        for c in range(n):
            dsrc[t, c] = stack_halves(out[:, c * 2 * HD : (c + 1) * 2 * HD]).astype(BF16)
        if t == 0:
            send_next(lambda peer: dsrc.at[0, peer], dbuf.at[0, me], 10)
        else:
            dbuf[1, me] = dsrc[1, me]
            send_peers(lambda peer: dsrc.at[1, peer], dbuf.at[1, me], 11)

    def total(t):
        terms = [dbuf[t, z].astype(F32) for z in range(n)]
        while len(terms) > 1:
            terms = [a + b for a, b in zip(terms[::2], terms[1::2])]
        return terms[0].astype(BF16).astype(F32)

    drain(state.at[0, others], recv_sem.at[0])
    project(0)

    @pl.when(seg > 0)
    def _():
        drain(state.at[1], recv_sem.at[1])

    project(1)
    attend(0)
    attend(1)
    loads[6].wait()
    combine(0)
    combine(1)

    drain(state.at[0, others], send_sem.at[0])
    for t in range(2):
        drain(qbuf.at[t, others], send_sem.at[2 + t])
        owned = lax.rem(me, 4) == 2 * t

        @pl.when(owned)
        def _():
            drain(kvsrc.at[t, pl.ds(0, 3)], send_sem.at[4 + t])

        @pl.when(jnp.logical_not(owned))
        def _():
            drain(kvsrc.at[t], send_sem.at[4 + t])

        drain(obuf.at[t, others], send_sem.at[6 + t])
        drain(stbuf.at[t, others], send_sem.at[8 + t])

    @pl.when(not_last)
    def _():
        drain(state.at[1], send_sem.at[1])
        drain(dbuf.at[0], send_sem.at[10])

    @pl.when(seg > 0)
    def _():
        drain(dbuf.at[0], recv_sem.at[10])

    hfin_ref[...] = unstack(state[1, me].astype(F32) + total(0)).astype(BF16)
    drain(dbuf.at[1, others], recv_sem.at[11])
    yfin_ref[...] = unstack(total(1)).astype(BF16)
    drain(dbuf.at[1, others], send_sem.at[11])


def solution(mesh):
    n = mesh.shape["tensor"]
    n_seg = mesh.shape["segment"]

    def local(h_init, y_init, norm_gain, w_query, w_kv, w_out, cache, lengths):
        hbm = pl.BlockSpec(memory_space=pltpu.HBM)
        vmem = pl.BlockSpec(memory_space=pltpu.VMEM)
        smem = pl.BlockSpec(memory_space=pltpu.SMEM)
        cache = jnp.transpose(cache, (0, 2, 1, 3))
        tile = (ROWS2, HD)
        return pl.pallas_call(
            functools.partial(kernel, n, n_seg),
            out_shape=(
                jax.ShapeDtypeStruct(h_init.shape, BF16),
                jax.ShapeDtypeStruct(h_init.shape, BF16),
            ),
            in_specs=[hbm] * 7 + [smem],
            out_specs=(vmem, vmem),
            scratch_shapes=[
                pltpu.VMEM(h_init.shape, BF16),
                pltpu.VMEM(y_init.shape, BF16),
                pltpu.VMEM(norm_gain.shape, BF16),
                pltpu.VMEM(w_query.shape, BF16),
                pltpu.VMEM(w_kv.shape, BF16),
                pltpu.VMEM(w_out.shape, BF16),
                pltpu.VMEM(cache.shape, BF16),
                pltpu.VMEM((2,) + tile, BF16),
                pltpu.VMEM((2, n) + tile, BF16),
                pltpu.VMEM((n, MB, 2 * HD), BF16),
                pltpu.VMEM(tile, F32),
                pltpu.VMEM(tile, F32),
                pltpu.VMEM((2,) + tile, BF16),
                pltpu.VMEM((2, n) + tile, BF16),
                pltpu.VMEM((MB * 2 * KVH, HD), F32),
                pltpu.VMEM((2, 4) + tile, BF16),
                pltpu.VMEM((2, n) + tile, BF16),
                pltpu.VMEM((2, ROWS2 * KVH * 16, HD), F32),
                pltpu.VMEM((ROWS2, KVH * 16, HD), BF16),
                pltpu.VMEM((ROWS2, KVH * 16, HD), BF16),
                pltpu.VMEM((MB * HEADS, HD), F32),
                pltpu.VMEM((MB * HEADS, HD), F32),
                pltpu.VMEM((2, n) + tile, BF16),
                pltpu.VMEM((2, n) + tile, BF16),
                pltpu.VMEM((2, n, 1, HD), F32),
                pltpu.VMEM((2, n, 1, HD), F32),
                pltpu.VMEM((2, n) + tile, BF16),
                pltpu.VMEM((2, n) + tile, BF16),
                pltpu.SemaphoreType.DMA((7,)),
                pltpu.SemaphoreType.DMA((12,)),
                pltpu.SemaphoreType.DMA((12,)),
            ],
            compiler_params=pltpu.CompilerParams(
                collective_id=0, has_side_effects=True, vmem_limit_bytes=60 << 20
            ),
        )(h_init, y_init, norm_gain, w_query, w_kv, w_out, cache, lengths)

    return jax.shard_map(
        local,
        mesh=mesh,
        in_specs=(
            P("segment", "tensor"),
            P("segment", "tensor"),
            P("segment", None),
            P("segment", None, "tensor"),
            P("segment", "tensor", None),
            P("segment", "tensor", None),
            P("segment", None, "tensor", None),
            P(),
        ),
        out_specs=(P("segment", "tensor"), P("segment", "tensor")),
        check_vma=False,
    )
```

```python
import functools
import math

import jax
import jax.numpy as jnp
from jax import lax
from jax.experimental import pallas as pl
from jax.experimental.pallas import tpu as pltpu
from jax.sharding import PartitionSpec as P

HEADS = 32
KVH = 4
HD = 128
TICKS = 2
MB = 8
ROWS2 = TICKS * MB
THETA = 500000.0
EPS = 1e-05
MASKED = -1e30
BIG = 1 << 30
MESH = pl.DeviceIdType.MESH
F32 = jnp.float32
BF16 = jnp.bfloat16


def far_first(i, me, n):
    d = n // 2 - (i + 1) // 2
    off = jnp.where(lax.rem(i, 2) == 1, d, n - d)
    return lax.rem(me + off, n)


def drain(ref, sem):
    pltpu.make_async_copy(ref, ref, sem).wait()


def stack_halves(v):
    return jnp.concatenate([v[:, :HD], v[:, HD:]], axis=0)


def unstack(v):
    return jnp.concatenate([v[:MB], v[MB:]], axis=1)


def kernel(
    n, n_seg, h_hbm, y_hbm, gain_hbm, wq_hbm, wkv_hbm, wo_hbm, cache_hbm, len_hbm,
    res_ref,
    h_in, y_in, gain, wq, wkv, wo, cache, len_ref,
    ssrc_state, state, nbuf, cosb, sinb,
    qsrc, qbuf, kvt32, kvsrc, kvbuf, kvt, kbuf, vbuf, qt, ot,
    osrc, obuf, stsrc, stbuf, dsrc, dbuf, waiting,
    load_sem, send_sem, recv_sem,
):
    me = lax.axis_index("tensor")
    seg = lax.axis_index("segment")
    first = seg == 0
    not_last = seg < n_seg - 1
    span = cache_hbm.shape[1]
    slots = KVH * 16
    others = pl.ds(0, n - 1)

    barrier = pltpu.get_barrier_semaphore()

    def tell(i, carry):
        pl.semaphore_signal(
            barrier, 1, device_id={"tensor": far_first(i, me, n)}, device_id_type=MESH
        )
        return carry

    lax.fori_loop(0, n - 1, tell, 0)

    @pl.when(seg > 0)
    def _():
        pl.semaphore_signal(
            barrier, 1, device_id={"segment": seg - 1, "tensor": me}, device_id_type=MESH
        )

    loads = [
        pltpu.make_async_copy(src, dst, load_sem.at[k])
        for k, (src, dst) in enumerate(
            [
                (h_hbm, h_in), (y_hbm, y_in), (gain_hbm, gain), (cache_hbm, cache),
                (wkv_hbm, wkv), (wq_hbm, wq), (wo_hbm, wo), (len_hbm, len_ref),
            ]
        )
    ]
    for load in loads:
        load.start()
    loads[0].wait()
    loads[1].wait()

    def send_peers(*sends):
        def step(i, carry):
            peer = far_first(i, me, n)
            for src_of, dst, sems in sends:
                pltpu.make_async_remote_copy(
                    src_of(peer), dst, send_sem.at[sems], recv_sem.at[sems],
                    device_id={"tensor": peer}, device_id_type=MESH,
                ).start()
            return carry

        lax.fori_loop(0, n - 1, step, 0)

    def pass_on(src, dst, sems):
        return pltpu.make_async_remote_copy(
            src, dst, send_sem.at[sems], recv_sem.at[sems],
            device_id={"segment": seg + 1, "tensor": me}, device_id_type=MESH,
        )

    h32 = h_in[...].astype(F32)
    a32 = (h32 + y_in[...].astype(F32)).astype(BF16).astype(F32)
    h_block = stack_halves(h32).astype(BF16)
    ssrc_state[0] = h_block
    ssrc_state[1] = stack_halves(a32).astype(BF16)
    state[0, me] = h_block

    pl.semaphore_wait(barrier, jnp.where(not_last, n, n - 1))

    @pl.when(not_last)
    def _():
        pass_on(ssrc_state.at[1], state.at[1, me], 12).start()

    send_peers((lambda peer: ssrc_state.at[0], state.at[0, me], 0))

    @pl.when(seg > 0)
    def _():
        drain(ssrc_state.at[1], recv_sem.at[12])
        send_peers((lambda peer: state.at[1, me], state.at[1, me], 1))


    loads[7].wait()
    row16 = lax.broadcasted_iota(jnp.int32, (ROWS2, HD), 0)
    lane16 = lax.broadcasted_iota(jnp.int32, (ROWS2, HD), 1)
    base1 = jnp.maximum(seg - 1, 0) * MB
    seen = [len_ref[seg * MB + b] for b in range(MB)] + [
        jnp.where(first, 0, len_ref[base1 + b]) for b in range(MB)
    ]
    seen_rows = jnp.zeros((ROWS2, HD), jnp.int32)
    for b in range(ROWS2):
        seen_rows = jnp.where(row16 == b, seen[b], seen_rows)
    half_lane = jnp.where(lane16 < HD // 2, lane16, lane16 - HD // 2)
    freqs = jnp.exp(-math.log(THETA) * (2.0 * half_lane.astype(F32) / HD))
    angles = seen_rows.astype(F32) * freqs
    sines = jnp.sin(angles)
    cosb[...] = jnp.cos(angles)
    sinb[...] = jnp.where(lane16 < HD // 2, -sines, sines)
    loads[3].wait()
    for p in range(16):
        for g in range(KVH):
            for part in range(2):
                if p < span:
                    col = (part * KVH + g) * HD
                    v = cache[0, p, :, col : col + HD].astype(F32)
                else:
                    v = jnp.zeros((ROWS2, HD), F32)
                kvt[part, pl.ds(g * 16 + p, ROWS2, stride=slots), :] = v
    for b in range(ROWS2):
        for part, dst in enumerate((kbuf, vbuf)):
            dst[b] = kvt[part, b * slots : (b + 1) * slots, :].astype(BF16)
    loads[2].wait()

    @pl.when(first)
    def _():
        state[1] = jnp.zeros_like(state[1])
        waiting[1] = jnp.zeros_like(waiting[1])

    loads[4].wait()
    loads[5].wait()
    jrow = lax.broadcasted_iota(jnp.int32, (HEADS, slots), 0)
    kcol = lax.broadcasted_iota(jnp.int32, (HEADS, slots), 1)
    same = lax.rem(jrow, 16) // 4 == kcol // 16
    slot = lax.rem(kcol, 16)
    place = jnp.where(same & (slot < span), me * span + slot, BIG)
    own_slot = same & (slot == span)
    lane32 = lax.broadcasted_iota(jnp.int32, (HEADS, HD), 1)
    krow = lax.broadcasted_iota(jnp.int32, (slots, HD), 0)
    scale = HD ** (-0.5)

    def project(t):
        chunks = []
        for z in range(n):
            v = state[t, z].astype(F32)
            chunks += [v[:MB], v[MB:]]
        squares = [c * c for c in chunks]
        while len(squares) > 1:
            squares = [a + b for a, b in zip(squares[::2], squares[1::2])]
        mean = jnp.sum(squares[0], axis=-1, keepdims=True) / (n * 2 * HD)
        inv = lax.rsqrt(mean + EPS)
        normed = []
        for k, c in enumerate(chunks):
            g = gain[0:1, k * HD : (k + 1) * HD].astype(F32)
            normed.append((c * inv * g).astype(BF16))
        for z in range(n):
            nbuf[z] = jnp.concatenate(normed[2 * z : 2 * z + 2], axis=1)
        kv = jnp.dot(nbuf[me], wkv[0], preferred_element_type=F32)
        for c in range(2 * KVH):
            kvt32[pl.ds(c, MB, stride=2 * KVH), :] = kv[:, c * HD : (c + 1) * HD]
        for o in range(4):
            kvsrc[t, o] = kvt32[o * 16 : (o + 1) * 16, :].astype(BF16)
        q32 = jnp.dot(jnp.concatenate(normed, axis=1), wq[0], preferred_element_type=F32)
        cosine = cosb[t * MB : (t + 1) * MB]
        sine = sinb[t * MB : (t + 1) * MB]
        turned = []
        for i in range(2):
            v = q32[:, i * HD : (i + 1) * HD]
            turned.append(v * cosine + pltpu.roll(v, HD // 2, 1) * sine)
        q = jnp.concatenate(turned, axis=0).astype(BF16)
        qsrc[t] = q
        qbuf[t, me] = q
        for o in range(4):
            owner = 4 * o + 2 * t

            @pl.when(me == owner)
            def _():
                kvbuf[t, owner] = kvsrc[t, o]

            @pl.when(me != owner)
            def _():
                pltpu.make_async_remote_copy(
                    kvsrc.at[t, o], kvbuf.at[t, me], send_sem.at[4 + t], recv_sem.at[4 + t],
                    device_id={"tensor": owner}, device_id_type=MESH,
                ).start()

        send_peers((lambda peer: qsrc.at[t], qbuf.at[t, me], 2 + t))

    def attend(t):
        @pl.when(lax.rem(me, 4) == 2 * t)
        def _():
            drain(kvbuf.at[t, others], recv_sem.at[4 + t])
            terms = [kvbuf[t, z].astype(F32) for z in range(n)]
            while len(terms) > 1:
                terms = [a + b for a, b in zip(terms[::2], terms[1::2])]
            fresh = terms[0]
            rolled = pltpu.roll(fresh, HD // 2, 1)
            for j in range(2):
                row = t * MB + (me // 4) * 2 + j
                at = j * 2 * KVH
                keys = (
                    fresh[at : at + KVH] * cosb[pl.ds(row, 1), :]
                    + rolled[at : at + KVH] * sinb[pl.ds(row, 1), :]
                )
                for dst, val in ((kbuf, keys), (vbuf, fresh[at + KVH : at + 2 * KVH])):
                    spread = jnp.concatenate(
                        [jnp.broadcast_to(val[g : g + 1], (16, HD)) for g in range(KVH)], axis=0
                    )
                    old = dst[row].astype(F32)
                    dst[row] = jnp.where(lax.rem(krow, 16) == span, spread, old).astype(BF16)

        drain(qbuf.at[t, others], recv_sem.at[2 + t])
        for r in range(n):
            v = qbuf[t, r].astype(F32)
            for i in range(2):
                qt[pl.ds(i * n + r, MB, stride=2 * n), :] = v[i * MB : (i + 1) * MB]
        scores = [
            lax.dot_general(
                qt[b * HEADS : (b + 1) * HEADS, :].astype(BF16),
                kbuf[t * MB + b],
                (((1,), (1,)), ((), ())),
                preferred_element_type=F32,
            )
            for b in range(MB)
        ]
        stats = jnp.zeros((HEADS, HD), F32)
        weights = []
        for b in range(MB):
            own_place = jnp.where(me == 4 * (b // 2) + 2 * t, -1, BIG)
            valid = jnp.where(own_slot, own_place, place) < seen[t * MB + b]
            s = jnp.where(valid, scores[b] * scale, MASKED)
            peak = jnp.max(s, axis=-1, keepdims=True)
            w = jnp.where(valid, jnp.exp(s - peak), 0.0)
            total = jnp.sum(w, axis=-1, keepdims=True)
            weights.append(w.astype(BF16))
            stats = jnp.where(lane32 == b, peak, stats)
            stats = jnp.where(lane32 == MB + b, total, stats)
        for b in range(MB):
            ot[b * HEADS : (b + 1) * HEADS, :] = jnp.dot(
                weights[b], vbuf[t * MB + b], preferred_element_type=F32
            )
        packed = jnp.where(lane32[:n] < 2 * MB, stats[:n], pltpu.roll(stats[n:], 2 * MB, 1))
        for r in range(n):
            stsrc[t, r] = packed[r : r + 1, :]
            osrc[t, r] = jnp.concatenate(
                [ot[pl.ds(i * n + r, MB, stride=2 * n), :] for i in range(2)], axis=0
            ).astype(BF16)
        obuf[t, me] = osrc[t, me]
        stbuf[t, me] = stsrc[t, me]
        send_peers(
            (lambda peer: osrc.at[t, peer], obuf.at[t, me], 6 + t),
            (lambda peer: stsrc.at[t, peer], stbuf.at[t, me], 8 + t),
        )

    def combine(t):
        drain(stbuf.at[t, others], recv_sem.at[8 + t])
        by_row = jnp.transpose(jnp.concatenate([stbuf[t, r] for r in range(n)], axis=0))
        shares = []
        for i in range(2):
            peaks = by_row[i * 16 : i * 16 + 8]
            totals = by_row[i * 16 + 8 : i * 16 + 16]
            scales = jnp.exp(peaks - jnp.max(peaks, axis=-1, keepdims=True))
            shares.append(scales / jnp.sum(scales * totals, axis=-1, keepdims=True))
        share = jnp.concatenate(shares, axis=0)
        drain(obuf.at[t, others], recv_sem.at[6 + t])
        terms = [obuf[t, r].astype(F32) * share[:, r : r + 1] for r in range(n)]
        while len(terms) > 1:
            terms = [a + b for a, b in zip(terms[::2], terms[1::2])]
        ctx = unstack(terms[0]).astype(BF16)
        out = jnp.dot(ctx, wo[0], preferred_element_type=F32)
        for c in range(n):
            dsrc[t, c] = stack_halves(out[:, c * 2 * HD : (c + 1) * 2 * HD]).astype(BF16)
        dbuf[t, me] = dsrc[t, me]
        send_peers((lambda peer: dsrc.at[t, peer], dbuf.at[t, me], 10 + t))

    def total(t):
        drain(dbuf.at[t, others], recv_sem.at[10 + t])
        terms = [dbuf[t, z].astype(F32) for z in range(n)]
        while len(terms) > 1:
            terms = [a + b for a, b in zip(terms[::2], terms[1::2])]
        return terms[0].astype(BF16)

    drain(state.at[0, others], recv_sem.at[0])
    project(0)

    @pl.when(seg > 0)
    def _():
        drain(state.at[1, others], recv_sem.at[1])

    project(1)
    attend(0)
    attend(1)
    loads[6].wait()
    combine(0)
    combine(1)

    waiting[0] = total(0)

    @pl.when(not_last)
    def _():
        pass_on(waiting.at[0], waiting.at[1], 13).start()

    drain(state.at[0, others], send_sem.at[0])
    for t in range(2):
        drain(qbuf.at[t, others], send_sem.at[2 + t])
        owned = lax.rem(me, 4) == 2 * t

        @pl.when(owned)
        def _():
            drain(kvsrc.at[t, pl.ds(0, 3)], send_sem.at[4 + t])

        @pl.when(jnp.logical_not(owned))
        def _():
            drain(kvsrc.at[t], send_sem.at[4 + t])

        drain(obuf.at[t, others], send_sem.at[6 + t])
        drain(stbuf.at[t, others], send_sem.at[8 + t])
    drain(dbuf.at[0, others], send_sem.at[10])

    @pl.when(seg > 0)
    def _():
        drain(state.at[1, others], send_sem.at[1])

    res_ref[1] = unstack(total(1).astype(F32)).astype(BF16)

    @pl.when(seg > 0)
    def _():
        drain(waiting.at[1], recv_sem.at[13])

    res_ref[0] = unstack(state[1, me].astype(F32) + waiting[1].astype(F32)).astype(BF16)
    drain(dbuf.at[1, others], send_sem.at[11])

    @pl.when(not_last)
    def _():
        drain(ssrc_state.at[1], send_sem.at[12])
        drain(waiting.at[0], send_sem.at[13])


def solution(mesh):
    n = mesh.shape["tensor"]
    n_seg = mesh.shape["segment"]

    def local(h_init, y_init, norm_gain, w_query, w_kv, w_out, cache, lengths):
        hbm = pl.BlockSpec(memory_space=pltpu.HBM)
        vmem = pl.BlockSpec(memory_space=pltpu.VMEM)
        cache = jnp.transpose(cache, (0, 2, 1, 3))
        tile = (ROWS2, HD)
        both = pl.pallas_call(
            functools.partial(kernel, n, n_seg),
            out_shape=jax.ShapeDtypeStruct((2,) + h_init.shape, BF16),
            in_specs=[hbm] * 8,
            out_specs=vmem,
            scratch_shapes=[
                pltpu.VMEM(h_init.shape, BF16),
                pltpu.VMEM(y_init.shape, BF16),
                pltpu.VMEM(norm_gain.shape, BF16),
                pltpu.VMEM(w_query.shape, BF16),
                pltpu.VMEM(w_kv.shape, BF16),
                pltpu.VMEM(w_out.shape, BF16),
                pltpu.VMEM(cache.shape, BF16),
                pltpu.SMEM(lengths.shape, jnp.int32),
                pltpu.VMEM((2,) + tile, BF16),
                pltpu.VMEM((2, n) + tile, BF16),
                pltpu.VMEM((n, MB, 2 * HD), BF16),
                pltpu.VMEM(tile, F32),
                pltpu.VMEM(tile, F32),
                pltpu.VMEM((2,) + tile, BF16),
                pltpu.VMEM((2, n) + tile, BF16),
                pltpu.VMEM((MB * 2 * KVH, HD), F32),
                pltpu.VMEM((2, 4) + tile, BF16),
                pltpu.VMEM((2, n) + tile, BF16),
                pltpu.VMEM((2, ROWS2 * KVH * 16, HD), F32),
                pltpu.VMEM((ROWS2, KVH * 16, HD), BF16),
                pltpu.VMEM((ROWS2, KVH * 16, HD), BF16),
                pltpu.VMEM((MB * HEADS, HD), F32),
                pltpu.VMEM((MB * HEADS, HD), F32),
                pltpu.VMEM((2, n) + tile, BF16),
                pltpu.VMEM((2, n) + tile, BF16),
                pltpu.VMEM((2, n, 1, HD), F32),
                pltpu.VMEM((2, n, 1, HD), F32),
                pltpu.VMEM((2, n) + tile, BF16),
                pltpu.VMEM((2, n) + tile, BF16),
                pltpu.VMEM((2,) + tile, BF16),
                pltpu.SemaphoreType.DMA((8,)),
                pltpu.SemaphoreType.DMA((14,)),
                pltpu.SemaphoreType.DMA((14,)),
            ],
            compiler_params=pltpu.CompilerParams(
                collective_id=0, has_side_effects=True, vmem_limit_bytes=60 << 20
            ),
        )(h_init, y_init, norm_gain, w_query, w_kv, w_out, cache, lengths)
        return both[0], both[1]

    return jax.shard_map(
        local,
        mesh=mesh,
        in_specs=(
            P("segment", "tensor"),
            P("segment", "tensor"),
            P("segment", None),
            P("segment", None, "tensor"),
            P("segment", "tensor", None),
            P("segment", "tensor", None),
            P("segment", None, "tensor", None),
            P(),
        ),
        out_specs=(P("segment", "tensor"), P("segment", "tensor")),
        check_vma=False,
    )
```

```python
import functools
import math

import jax
import jax.numpy as jnp
from jax import lax
from jax.experimental import pallas as pl
from jax.experimental.pallas import tpu as pltpu
from jax.sharding import PartitionSpec as P

HEADS = 32
KVH = 4
HD = 128
TICKS = 2
MB = 8
ROWS2 = TICKS * MB
THETA = 500000.0
EPS = 1e-05
MASKED = -1e30
BIG = 1 << 30
MESH = pl.DeviceIdType.MESH
F32 = jnp.float32
BF16 = jnp.bfloat16


def far_first(i, me, n):
    d = n // 2 - (i + 1) // 2
    off = jnp.where(lax.rem(i, 2) == 1, d, n - d)
    return lax.rem(me + off, n)


def drain(ref, sem):
    pltpu.make_async_copy(ref, ref, sem).wait()


def stack_halves(v):
    return jnp.concatenate([v[:, :HD], v[:, HD:]], axis=0)


def unstack(v):
    return jnp.concatenate([v[:MB], v[MB:]], axis=1)


def kernel(
    n, n_seg, h_hbm, y_hbm, gain_hbm, wq_hbm, wkv_hbm, wo_hbm, cache_hbm, len_hbm,
    res_ref,
    h_in, y_in, gain, wq, wkv, wo, cache, len_ref,
    ssrc_state, state, nbuf, cosb, sinb,
    qsrc, qbuf, kvt32, kvsrc, kvbuf, kvt, kbuf, vbuf, qt, ot,
    osrc, obuf, stsrc, stbuf, dsrc, dbuf, waiting,
    load_sem, send_sem, recv_sem,
):
    me = lax.axis_index("tensor")
    seg = lax.axis_index("segment")
    first = seg == 0
    not_last = seg < n_seg - 1
    span = cache_hbm.shape[1]
    slots = KVH * 16
    others = pl.ds(0, n - 1)

    reach = n // 4
    near = [sign * d for d in range(reach, 0, -1) for sign in (1, -1)]

    def at(off):
        return lax.rem(me + (off + n), n)

    barrier = pltpu.get_barrier_semaphore()

    for off in near:
        pl.semaphore_signal(barrier, 1, device_id={"tensor": at(off)}, device_id_type=MESH)

    @pl.when(seg > 0)
    def _():
        pl.semaphore_signal(
            barrier, 1, device_id={"segment": seg - 1, "tensor": me}, device_id_type=MESH
        )

    loads = [
        pltpu.make_async_copy(src, dst, load_sem.at[k])
        for k, (src, dst) in enumerate(
            [
                (h_hbm, h_in), (y_hbm, y_in), (gain_hbm, gain), (cache_hbm, cache),
                (wkv_hbm, wkv), (wq_hbm, wq), (wo_hbm, wo), (len_hbm, len_ref),
            ]
        )
    ]
    for load in loads:
        load.start()
    loads[0].wait()
    loads[1].wait()

    def send_peers(*sends):
        def step(i, carry):
            peer = far_first(i, me, n)
            for src_of, dst, sems in sends:
                pltpu.make_async_remote_copy(
                    src_of(peer), dst, send_sem.at[sems], recv_sem.at[sems],
                    device_id={"tensor": peer}, device_id_type=MESH,
                ).start()
            return carry

        lax.fori_loop(0, n - 1, step, 0)

    def pass_on(src, dst, sems):
        return pltpu.make_async_remote_copy(
            src, dst, send_sem.at[sems], recv_sem.at[sems],
            device_id={"segment": seg + 1, "tensor": me}, device_id_type=MESH,
        )

    h32 = h_in[...].astype(F32)
    a32 = (h32 + y_in[...].astype(F32)).astype(BF16).astype(F32)
    h_block = stack_halves(h32).astype(BF16)
    ssrc_state[0] = h_block
    ssrc_state[1] = stack_halves(a32).astype(BF16)
    state[0, me] = h_block

    pl.semaphore_wait(barrier, jnp.where(not_last, 2 * reach + 1, 2 * reach))

    @pl.when(not_last)
    def _():
        pass_on(ssrc_state.at[1], state.at[1, me], 12).start()

    def spread(t, src):
        for off in near:
            sem = 14 + t if off == reach else 16 + t if off == -reach else t
            pltpu.make_async_remote_copy(
                src, state.at[t, me], send_sem.at[t], recv_sem.at[sem],
                device_id={"tensor": at(off)}, device_id_type=MESH,
            ).start()

    def relay(t):
        for sign, sem in ((1, 14 + t), (-1, 16 + t)):
            block = state.at[t, at(-sign * reach)]
            drain(block, recv_sem.at[sem])
            for d in range(reach if sign == 1 else reach - 1, 0, -1):
                pltpu.make_async_remote_copy(
                    block, block, send_sem.at[t], recv_sem.at[18 + t],
                    device_id={"tensor": at(sign * d)}, device_id_type=MESH,
                ).start()

    def gathered(t):
        drain(state.at[t, pl.ds(0, 2 * reach - 2)], recv_sem.at[t])
        drain(state.at[t, pl.ds(0, 2 * reach - 1)], recv_sem.at[18 + t])

    spread(0, ssrc_state.at[0])

    loads[7].wait()
    row16 = lax.broadcasted_iota(jnp.int32, (ROWS2, HD), 0)
    lane16 = lax.broadcasted_iota(jnp.int32, (ROWS2, HD), 1)
    base1 = jnp.maximum(seg - 1, 0) * MB
    seen = [len_ref[seg * MB + b] for b in range(MB)] + [
        jnp.where(first, 0, len_ref[base1 + b]) for b in range(MB)
    ]
    seen_rows = jnp.zeros((ROWS2, HD), jnp.int32)
    for b in range(ROWS2):
        seen_rows = jnp.where(row16 == b, seen[b], seen_rows)
    half_lane = jnp.where(lane16 < HD // 2, lane16, lane16 - HD // 2)
    freqs = jnp.exp(-math.log(THETA) * (2.0 * half_lane.astype(F32) / HD))
    angles = seen_rows.astype(F32) * freqs
    sines = jnp.sin(angles)
    cosb[...] = jnp.cos(angles)
    sinb[...] = jnp.where(lane16 < HD // 2, -sines, sines)
    @pl.when(seg > 0)
    def _():
        drain(ssrc_state.at[1], recv_sem.at[12])
        spread(1, state.at[1, me])

    relay(0)

    @pl.when(seg > 0)
    def _():
        relay(1)

    loads[2].wait()

    @pl.when(first)
    def _():
        state[1] = jnp.zeros_like(state[1])
        waiting[1] = jnp.zeros_like(waiting[1])

    loads[4].wait()
    loads[5].wait()
    jrow = lax.broadcasted_iota(jnp.int32, (HEADS, slots), 0)
    kcol = lax.broadcasted_iota(jnp.int32, (HEADS, slots), 1)
    same = lax.rem(jrow, 16) // 4 == kcol // 16
    slot = lax.rem(kcol, 16)
    place = jnp.where(same & (slot < span), me * span + slot, BIG)
    own_slot = same & (slot == span)
    lane32 = lax.broadcasted_iota(jnp.int32, (HEADS, HD), 1)
    krow = lax.broadcasted_iota(jnp.int32, (slots, HD), 0)
    scale = HD ** (-0.5)

    def project(t):
        chunks = []
        for z in range(n):
            v = state[t, z].astype(F32)
            chunks += [v[:MB], v[MB:]]
        squares = [c * c for c in chunks]
        while len(squares) > 1:
            squares = [a + b for a, b in zip(squares[::2], squares[1::2])]
        mean = jnp.sum(squares[0], axis=-1, keepdims=True) / (n * 2 * HD)
        inv = lax.rsqrt(mean + EPS)
        normed = []
        for k, c in enumerate(chunks):
            g = gain[0:1, k * HD : (k + 1) * HD].astype(F32)
            normed.append((c * inv * g).astype(BF16))
        for z in range(n):
            nbuf[z] = jnp.concatenate(normed[2 * z : 2 * z + 2], axis=1)
        kv = jnp.dot(nbuf[me], wkv[0], preferred_element_type=F32)
        for c in range(2 * KVH):
            kvt32[pl.ds(c, MB, stride=2 * KVH), :] = kv[:, c * HD : (c + 1) * HD]
        for o in range(4):
            kvsrc[t, o] = kvt32[o * 16 : (o + 1) * 16, :].astype(BF16)
        q32 = jnp.dot(jnp.concatenate(normed, axis=1), wq[0], preferred_element_type=F32)
        cosine = cosb[t * MB : (t + 1) * MB]
        sine = sinb[t * MB : (t + 1) * MB]
        turned = []
        for i in range(2):
            v = q32[:, i * HD : (i + 1) * HD]
            turned.append(v * cosine + pltpu.roll(v, HD // 2, 1) * sine)
        q = jnp.concatenate(turned, axis=0).astype(BF16)
        qsrc[t] = q
        qbuf[t, me] = q
        for o in range(4):
            owner = 4 * o + 2 * t

            @pl.when(me == owner)
            def _():
                kvbuf[t, owner] = kvsrc[t, o]

            @pl.when(me != owner)
            def _():
                pltpu.make_async_remote_copy(
                    kvsrc.at[t, o], kvbuf.at[t, me], send_sem.at[4 + t], recv_sem.at[4 + t],
                    device_id={"tensor": owner}, device_id_type=MESH,
                ).start()

        send_peers((lambda peer: qsrc.at[t], qbuf.at[t, me], 2 + t))

    def attend(t):
        @pl.when(lax.rem(me, 4) == 2 * t)
        def _():
            drain(kvbuf.at[t, others], recv_sem.at[4 + t])
            terms = [kvbuf[t, z].astype(F32) for z in range(n)]
            while len(terms) > 1:
                terms = [a + b for a, b in zip(terms[::2], terms[1::2])]
            fresh = terms[0]
            rolled = pltpu.roll(fresh, HD // 2, 1)
            for j in range(2):
                row = t * MB + (me // 4) * 2 + j
                at = j * 2 * KVH
                keys = (
                    fresh[at : at + KVH] * cosb[pl.ds(row, 1), :]
                    + rolled[at : at + KVH] * sinb[pl.ds(row, 1), :]
                )
                for dst, val in ((kbuf, keys), (vbuf, fresh[at + KVH : at + 2 * KVH])):
                    spread = jnp.concatenate(
                        [jnp.broadcast_to(val[g : g + 1], (16, HD)) for g in range(KVH)], axis=0
                    )
                    old = dst[row].astype(F32)
                    dst[row] = jnp.where(lax.rem(krow, 16) == span, spread, old).astype(BF16)

        drain(qbuf.at[t, others], recv_sem.at[2 + t])
        for r in range(n):
            v = qbuf[t, r].astype(F32)
            for i in range(2):
                qt[pl.ds(i * n + r, MB, stride=2 * n), :] = v[i * MB : (i + 1) * MB]
        scores = [
            lax.dot_general(
                qt[b * HEADS : (b + 1) * HEADS, :].astype(BF16),
                kbuf[t * MB + b],
                (((1,), (1,)), ((), ())),
                preferred_element_type=F32,
            )
            for b in range(MB)
        ]
        stats = jnp.zeros((HEADS, HD), F32)
        weights = []
        for b in range(MB):
            own_place = jnp.where(me == 4 * (b // 2) + 2 * t, -1, BIG)
            valid = jnp.where(own_slot, own_place, place) < seen[t * MB + b]
            s = jnp.where(valid, scores[b] * scale, MASKED)
            peak = jnp.max(s, axis=-1, keepdims=True)
            w = jnp.where(valid, jnp.exp(s - peak), 0.0)
            total = jnp.sum(w, axis=-1, keepdims=True)
            weights.append(w.astype(BF16))
            stats = jnp.where(lane32 == b, peak, stats)
            stats = jnp.where(lane32 == MB + b, total, stats)
        for b in range(MB):
            ot[b * HEADS : (b + 1) * HEADS, :] = jnp.dot(
                weights[b], vbuf[t * MB + b], preferred_element_type=F32
            )
        packed = jnp.where(lane32[:n] < 2 * MB, stats[:n], pltpu.roll(stats[n:], 2 * MB, 1))
        for r in range(n):
            stsrc[t, r] = packed[r : r + 1, :]
            osrc[t, r] = jnp.concatenate(
                [ot[pl.ds(i * n + r, MB, stride=2 * n), :] for i in range(2)], axis=0
            ).astype(BF16)
        obuf[t, me] = osrc[t, me]
        stbuf[t, me] = stsrc[t, me]
        send_peers(
            (lambda peer: osrc.at[t, peer], obuf.at[t, me], 6 + t),
            (lambda peer: stsrc.at[t, peer], stbuf.at[t, me], 8 + t),
        )

    def combine(t):
        drain(stbuf.at[t, others], recv_sem.at[8 + t])
        by_row = jnp.transpose(jnp.concatenate([stbuf[t, r] for r in range(n)], axis=0))
        shares = []
        for i in range(2):
            peaks = by_row[i * 16 : i * 16 + 8]
            totals = by_row[i * 16 + 8 : i * 16 + 16]
            scales = jnp.exp(peaks - jnp.max(peaks, axis=-1, keepdims=True))
            shares.append(scales / jnp.sum(scales * totals, axis=-1, keepdims=True))
        share = jnp.concatenate(shares, axis=0)
        drain(obuf.at[t, others], recv_sem.at[6 + t])
        terms = [obuf[t, r].astype(F32) * share[:, r : r + 1] for r in range(n)]
        while len(terms) > 1:
            terms = [a + b for a, b in zip(terms[::2], terms[1::2])]
        ctx = unstack(terms[0]).astype(BF16)
        out = jnp.dot(ctx, wo[0], preferred_element_type=F32)
        for c in range(n):
            dsrc[t, c] = stack_halves(out[:, c * 2 * HD : (c + 1) * 2 * HD]).astype(BF16)
        dbuf[t, me] = dsrc[t, me]
        send_peers((lambda peer: dsrc.at[t, peer], dbuf.at[t, me], 10 + t))

    def total(t):
        drain(dbuf.at[t, others], recv_sem.at[10 + t])
        terms = [dbuf[t, z].astype(F32) for z in range(n)]
        while len(terms) > 1:
            terms = [a + b for a, b in zip(terms[::2], terms[1::2])]
        return terms[0].astype(BF16)

    gathered(0)
    project(0)

    @pl.when(seg > 0)
    def _():
        gathered(1)

    project(1)

    loads[3].wait()
    for p in range(16):
        for g in range(KVH):
            for part in range(2):
                if p < span:
                    col = (part * KVH + g) * HD
                    v = cache[0, p, :, col : col + HD].astype(F32)
                else:
                    v = jnp.zeros((ROWS2, HD), F32)
                kvt[part, pl.ds(g * 16 + p, ROWS2, stride=slots), :] = v
    for b in range(ROWS2):
        for part, dst in enumerate((kbuf, vbuf)):
            dst[b] = kvt[part, b * slots : (b + 1) * slots, :].astype(BF16)

    attend(0)
    attend(1)
    loads[6].wait()
    combine(0)
    combine(1)

    waiting[0] = total(0)

    @pl.when(not_last)
    def _():
        pass_on(waiting.at[0], waiting.at[1], 13).start()

    drain(state.at[0, others], send_sem.at[0])
    for t in range(2):
        drain(qbuf.at[t, others], send_sem.at[2 + t])
        owned = lax.rem(me, 4) == 2 * t

        @pl.when(owned)
        def _():
            drain(kvsrc.at[t, pl.ds(0, 3)], send_sem.at[4 + t])

        @pl.when(jnp.logical_not(owned))
        def _():
            drain(kvsrc.at[t], send_sem.at[4 + t])

        drain(obuf.at[t, others], send_sem.at[6 + t])
        drain(stbuf.at[t, others], send_sem.at[8 + t])
    drain(dbuf.at[0, others], send_sem.at[10])

    @pl.when(seg > 0)
    def _():
        drain(state.at[1, others], send_sem.at[1])

    res_ref[1] = unstack(total(1).astype(F32)).astype(BF16)

    @pl.when(seg > 0)
    def _():
        drain(waiting.at[1], recv_sem.at[13])

    res_ref[0] = unstack(state[1, me].astype(F32) + waiting[1].astype(F32)).astype(BF16)
    drain(dbuf.at[1, others], send_sem.at[11])

    @pl.when(not_last)
    def _():
        drain(ssrc_state.at[1], send_sem.at[12])
        drain(waiting.at[0], send_sem.at[13])


def solution(mesh):
    n = mesh.shape["tensor"]
    n_seg = mesh.shape["segment"]

    def local(h_init, y_init, norm_gain, w_query, w_kv, w_out, cache, lengths):
        hbm = pl.BlockSpec(memory_space=pltpu.HBM)
        vmem = pl.BlockSpec(memory_space=pltpu.VMEM)
        cache = jnp.transpose(cache, (0, 2, 1, 3))
        tile = (ROWS2, HD)
        both = pl.pallas_call(
            functools.partial(kernel, n, n_seg),
            out_shape=jax.ShapeDtypeStruct((2,) + h_init.shape, BF16),
            in_specs=[hbm] * 8,
            out_specs=vmem,
            scratch_shapes=[
                pltpu.VMEM(h_init.shape, BF16),
                pltpu.VMEM(y_init.shape, BF16),
                pltpu.VMEM(norm_gain.shape, BF16),
                pltpu.VMEM(w_query.shape, BF16),
                pltpu.VMEM(w_kv.shape, BF16),
                pltpu.VMEM(w_out.shape, BF16),
                pltpu.VMEM(cache.shape, BF16),
                pltpu.SMEM(lengths.shape, jnp.int32),
                pltpu.VMEM((2,) + tile, BF16),
                pltpu.VMEM((2, n) + tile, BF16),
                pltpu.VMEM((n, MB, 2 * HD), BF16),
                pltpu.VMEM(tile, F32),
                pltpu.VMEM(tile, F32),
                pltpu.VMEM((2,) + tile, BF16),
                pltpu.VMEM((2, n) + tile, BF16),
                pltpu.VMEM((MB * 2 * KVH, HD), F32),
                pltpu.VMEM((2, 4) + tile, BF16),
                pltpu.VMEM((2, n) + tile, BF16),
                pltpu.VMEM((2, ROWS2 * KVH * 16, HD), F32),
                pltpu.VMEM((ROWS2, KVH * 16, HD), BF16),
                pltpu.VMEM((ROWS2, KVH * 16, HD), BF16),
                pltpu.VMEM((MB * HEADS, HD), F32),
                pltpu.VMEM((MB * HEADS, HD), F32),
                pltpu.VMEM((2, n) + tile, BF16),
                pltpu.VMEM((2, n) + tile, BF16),
                pltpu.VMEM((2, n, 1, HD), F32),
                pltpu.VMEM((2, n, 1, HD), F32),
                pltpu.VMEM((2, n) + tile, BF16),
                pltpu.VMEM((2, n) + tile, BF16),
                pltpu.VMEM((2,) + tile, BF16),
                pltpu.SemaphoreType.DMA((8,)),
                pltpu.SemaphoreType.DMA((20,)),
                pltpu.SemaphoreType.DMA((20,)),
            ],
            compiler_params=pltpu.CompilerParams(
                collective_id=0, has_side_effects=True, vmem_limit_bytes=60 << 20
            ),
        )(h_init, y_init, norm_gain, w_query, w_kv, w_out, cache, lengths)
        return both[0], both[1]

    return jax.shard_map(
        local,
        mesh=mesh,
        in_specs=(
            P("segment", "tensor"),
            P("segment", "tensor"),
            P("segment", None),
            P("segment", None, "tensor"),
            P("segment", "tensor", None),
            P("segment", "tensor", None),
            P("segment", None, "tensor", None),
            P(),
        ),
        out_specs=(P("segment", "tensor"), P("segment", "tensor")),
        check_vma=False,
    )
```

```python
import functools
import math

import jax
import jax.numpy as jnp
from jax import lax
from jax.experimental import pallas as pl
from jax.experimental.pallas import tpu as pltpu
from jax.sharding import PartitionSpec as P

HEADS = 32
KVH = 4
HD = 128
TICKS = 2
MB = 8
ROWS2 = TICKS * MB
THETA = 500000.0
EPS = 1e-05
MASKED = -1e30
BIG = 1 << 30
MESH = pl.DeviceIdType.MESH
F32 = jnp.float32
BF16 = jnp.bfloat16


def far_first(i, me, n):
    d = n // 2 - (i + 1) // 2
    off = jnp.where(lax.rem(i, 2) == 1, d, n - d)
    return lax.rem(me + off, n)


def drain(ref, sem):
    pltpu.make_async_copy(ref, ref, sem).wait()


def stack_halves(v):
    return jnp.concatenate([v[:, :HD], v[:, HD:]], axis=0)


def unstack(v):
    return jnp.concatenate([v[:MB], v[MB:]], axis=1)


def kernel(
    n, n_seg, h_hbm, y_hbm, gain_hbm, wq_hbm, wkv_hbm, wo_hbm, cache_hbm, len_hbm,
    res_ref,
    h_in, y_in, gain, wq, wkv, wo, cache, len_ref,
    ssrc_state, state, nbuf, cosb, sinb,
    qsrc, qbuf, kvt32, kvsrc, kvbuf, kvt, kbuf, vbuf, qt, ot,
    osrc, obuf, stsrc, stbuf, dsrc, dbuf, waiting,
    load_sem, send_sem, recv_sem,
):
    me = lax.axis_index("tensor")
    seg = lax.axis_index("segment")
    first = seg == 0
    not_last = seg < n_seg - 1
    span = cache_hbm.shape[1]
    slots = KVH * 16
    others = pl.ds(0, n - 1)

    reach = n // 4
    near = [sign * d for d in range(reach, 0, -1) for sign in (1, -1)]

    def at(off):
        return lax.rem(me + (off + n), n)

    loads = [
        pltpu.make_async_copy(src, dst, load_sem.at[k])
        for k, (src, dst) in enumerate(
            [
                (h_hbm, h_in), (y_hbm, y_in), (gain_hbm, gain), (cache_hbm, cache),
                (wkv_hbm, wkv), (wq_hbm, wq), (wo_hbm, wo), (len_hbm, len_ref),
            ]
        )
    ]
    loads[0].start()
    loads[1].start()

    barrier = pltpu.get_barrier_semaphore()

    for off in near:
        pl.semaphore_signal(barrier, 1, device_id={"tensor": at(off)}, device_id_type=MESH)

    @pl.when(seg > 0)
    def _():
        pl.semaphore_signal(
            barrier, 1, device_id={"segment": seg - 1, "tensor": me}, device_id_type=MESH
        )

    for load in loads[2:]:
        load.start()
    loads[0].wait()
    loads[1].wait()

    def send_peers(*sends):
        def step(i, carry):
            peer = far_first(i, me, n)
            for src_of, dst, sems in sends:
                pltpu.make_async_remote_copy(
                    src_of(peer), dst, send_sem.at[sems], recv_sem.at[sems],
                    device_id={"tensor": peer}, device_id_type=MESH,
                ).start()
            return carry

        lax.fori_loop(0, n - 1, step, 0, unroll=True)

    def pass_on(src, dst, sems):
        return pltpu.make_async_remote_copy(
            src, dst, send_sem.at[sems], recv_sem.at[sems],
            device_id={"segment": seg + 1, "tensor": me}, device_id_type=MESH,
        )

    h32 = h_in[...].astype(F32)
    a32 = (h32 + y_in[...].astype(F32)).astype(BF16).astype(F32)
    h_block = stack_halves(h32).astype(BF16)
    ssrc_state[0] = h_block
    ssrc_state[1] = stack_halves(a32).astype(BF16)
    state[0, me] = h_block

    pl.semaphore_wait(barrier, jnp.where(not_last, 2 * reach + 1, 2 * reach))

    @pl.when(not_last)
    def _():
        pass_on(ssrc_state.at[1], state.at[1, me], 12).start()

    def spread(t, src):
        for off in near:
            sem = 14 + t if off == reach else 16 + t if off == -reach else t
            pltpu.make_async_remote_copy(
                src, state.at[t, me], send_sem.at[t], recv_sem.at[sem],
                device_id={"tensor": at(off)}, device_id_type=MESH,
            ).start()

    def relay(t):
        for sign, sem in ((1, 14 + t), (-1, 16 + t)):
            block = state.at[t, at(-sign * reach)]
            drain(block, recv_sem.at[sem])
            for d in range(reach if sign == 1 else reach - 1, 0, -1):
                pltpu.make_async_remote_copy(
                    block, block, send_sem.at[t], recv_sem.at[18 + t],
                    device_id={"tensor": at(sign * d)}, device_id_type=MESH,
                ).start()

    def gathered(t):
        drain(state.at[t, pl.ds(0, 2 * reach - 2)], recv_sem.at[t])
        drain(state.at[t, pl.ds(0, 2 * reach - 1)], recv_sem.at[18 + t])

    spread(0, ssrc_state.at[0])

    loads[7].wait()
    row16 = lax.broadcasted_iota(jnp.int32, (ROWS2, HD), 0)
    lane16 = lax.broadcasted_iota(jnp.int32, (ROWS2, HD), 1)
    base1 = jnp.maximum(seg - 1, 0) * MB
    seen = [len_ref[seg * MB + b] for b in range(MB)] + [
        jnp.where(first, 0, len_ref[base1 + b]) for b in range(MB)
    ]
    seen_rows = jnp.zeros((ROWS2, HD), jnp.int32)
    for b in range(ROWS2):
        seen_rows = jnp.where(row16 == b, seen[b], seen_rows)
    half_lane = jnp.where(lane16 < HD // 2, lane16, lane16 - HD // 2)
    freqs = jnp.exp(-math.log(THETA) * (2.0 * half_lane.astype(F32) / HD))
    angles = seen_rows.astype(F32) * freqs
    sines = jnp.sin(angles)
    cosb[...] = jnp.cos(angles)
    sinb[...] = jnp.where(lane16 < HD // 2, -sines, sines)
    @pl.when(seg > 0)
    def _():
        drain(ssrc_state.at[1], recv_sem.at[12])
        spread(1, state.at[1, me])

    relay(0)

    @pl.when(seg > 0)
    def _():
        relay(1)

    loads[2].wait()

    @pl.when(first)
    def _():
        state[1] = jnp.zeros_like(state[1])
        waiting[1] = jnp.zeros_like(waiting[1])

    loads[4].wait()
    loads[5].wait()
    jrow = lax.broadcasted_iota(jnp.int32, (HEADS, slots), 0)
    kcol = lax.broadcasted_iota(jnp.int32, (HEADS, slots), 1)
    same = lax.rem(jrow, 16) // 4 == kcol // 16
    slot = lax.rem(kcol, 16)
    place = jnp.where(same & (slot < span), me * span + slot, BIG)
    own_slot = same & (slot == span)
    lane32 = lax.broadcasted_iota(jnp.int32, (HEADS, HD), 1)
    krow = lax.broadcasted_iota(jnp.int32, (slots, HD), 0)
    scale = HD ** (-0.5)

    def project(t):
        chunks = []
        for z in range(n):
            v = state[t, z].astype(F32)
            chunks += [v[:MB], v[MB:]]
        squares = [c * c for c in chunks]
        while len(squares) > 1:
            squares = [a + b for a, b in zip(squares[::2], squares[1::2])]
        mean = jnp.sum(squares[0], axis=-1, keepdims=True) / (n * 2 * HD)
        inv = lax.rsqrt(mean + EPS)
        normed = []
        for k, c in enumerate(chunks):
            g = gain[0:1, k * HD : (k + 1) * HD].astype(F32)
            normed.append((c * inv * g).astype(BF16))
        for z in range(n):
            nbuf[z] = jnp.concatenate(normed[2 * z : 2 * z + 2], axis=1)
        kv = jnp.dot(nbuf[me], wkv[0], preferred_element_type=F32)
        for c in range(2 * KVH):
            kvt32[pl.ds(c, MB, stride=2 * KVH), :] = kv[:, c * HD : (c + 1) * HD]
        for o in range(4):
            kvsrc[t, o] = kvt32[o * 16 : (o + 1) * 16, :].astype(BF16)
        q32 = jnp.dot(jnp.concatenate(normed, axis=1), wq[0], preferred_element_type=F32)
        cosine = cosb[t * MB : (t + 1) * MB]
        sine = sinb[t * MB : (t + 1) * MB]
        turned = []
        for i in range(2):
            v = q32[:, i * HD : (i + 1) * HD]
            turned.append(v * cosine + pltpu.roll(v, HD // 2, 1) * sine)
        q = jnp.concatenate(turned, axis=0).astype(BF16)
        qsrc[t] = q
        qbuf[t, me] = q
        for o in range(4):
            owner = 4 * o + 2 * t

            @pl.when(me == owner)
            def _():
                kvbuf[t, owner] = kvsrc[t, o]

            @pl.when(me != owner)
            def _():
                pltpu.make_async_remote_copy(
                    kvsrc.at[t, o], kvbuf.at[t, me], send_sem.at[4 + t], recv_sem.at[4 + t],
                    device_id={"tensor": owner}, device_id_type=MESH,
                ).start()

        send_peers((lambda peer: qsrc.at[t], qbuf.at[t, me], 2 + t))

    def attend(t):
        @pl.when(lax.rem(me, 4) == 2 * t)
        def _():
            drain(kvbuf.at[t, others], recv_sem.at[4 + t])
            terms = [kvbuf[t, z].astype(F32) for z in range(n)]
            while len(terms) > 1:
                terms = [a + b for a, b in zip(terms[::2], terms[1::2])]
            fresh = terms[0]
            rolled = pltpu.roll(fresh, HD // 2, 1)
            for j in range(2):
                row = t * MB + (me // 4) * 2 + j
                at = j * 2 * KVH
                keys = (
                    fresh[at : at + KVH] * cosb[pl.ds(row, 1), :]
                    + rolled[at : at + KVH] * sinb[pl.ds(row, 1), :]
                )
                for dst, val in ((kbuf, keys), (vbuf, fresh[at + KVH : at + 2 * KVH])):
                    spread = jnp.concatenate(
                        [jnp.broadcast_to(val[g : g + 1], (16, HD)) for g in range(KVH)], axis=0
                    )
                    old = dst[row].astype(F32)
                    dst[row] = jnp.where(lax.rem(krow, 16) == span, spread, old).astype(BF16)

        drain(qbuf.at[t, others], recv_sem.at[2 + t])
        for r in range(n):
            v = qbuf[t, r].astype(F32)
            for i in range(2):
                qt[pl.ds(i * n + r, MB, stride=2 * n), :] = v[i * MB : (i + 1) * MB]
        scores = [
            lax.dot_general(
                qt[b * HEADS : (b + 1) * HEADS, :].astype(BF16),
                kbuf[t * MB + b],
                (((1,), (1,)), ((), ())),
                preferred_element_type=F32,
            )
            for b in range(MB)
        ]
        stats = jnp.zeros((HEADS, HD), F32)
        weights = []
        for b in range(MB):
            own_place = jnp.where(me == 4 * (b // 2) + 2 * t, -1, BIG)
            valid = jnp.where(own_slot, own_place, place) < seen[t * MB + b]
            s = jnp.where(valid, scores[b] * scale, MASKED)
            peak = jnp.max(s, axis=-1, keepdims=True)
            w = jnp.where(valid, jnp.exp(s - peak), 0.0)
            total = jnp.sum(w, axis=-1, keepdims=True)
            weights.append(w.astype(BF16))
            stats = jnp.where(lane32 == b, peak, stats)
            stats = jnp.where(lane32 == MB + b, total, stats)
        for b in range(MB):
            ot[b * HEADS : (b + 1) * HEADS, :] = jnp.dot(
                weights[b], vbuf[t * MB + b], preferred_element_type=F32
            )
        packed = jnp.where(lane32[:n] < 2 * MB, stats[:n], pltpu.roll(stats[n:], 2 * MB, 1))
        for r in range(n):
            stsrc[t, r] = packed[r : r + 1, :]
            osrc[t, r] = jnp.concatenate(
                [ot[pl.ds(i * n + r, MB, stride=2 * n), :] for i in range(2)], axis=0
            ).astype(BF16)
        obuf[t, me] = osrc[t, me]
        stbuf[t, me] = stsrc[t, me]
        send_peers(
            (lambda peer: osrc.at[t, peer], obuf.at[t, me], 6 + t),
            (lambda peer: stsrc.at[t, peer], stbuf.at[t, me], 8 + t),
        )

    def combine(t):
        drain(stbuf.at[t, others], recv_sem.at[8 + t])
        by_row = jnp.transpose(jnp.concatenate([stbuf[t, r] for r in range(n)], axis=0))
        shares = []
        for i in range(2):
            peaks = by_row[i * 16 : i * 16 + 8]
            totals = by_row[i * 16 + 8 : i * 16 + 16]
            scales = jnp.exp(peaks - jnp.max(peaks, axis=-1, keepdims=True))
            shares.append(scales / jnp.sum(scales * totals, axis=-1, keepdims=True))
        share = jnp.concatenate(shares, axis=0)
        drain(obuf.at[t, others], recv_sem.at[6 + t])
        terms = [obuf[t, r].astype(F32) * share[:, r : r + 1] for r in range(n)]
        while len(terms) > 1:
            terms = [a + b for a, b in zip(terms[::2], terms[1::2])]
        ctx = unstack(terms[0]).astype(BF16)
        out = jnp.dot(ctx, wo[0], preferred_element_type=F32)
        for c in range(n):
            dsrc[t, c] = stack_halves(out[:, c * 2 * HD : (c + 1) * 2 * HD]).astype(BF16)
        dbuf[t, me] = dsrc[t, me]
        def step(peer, carry):
            @pl.when(peer != me)
            def _():
                pltpu.make_async_remote_copy(
                    dsrc.at[t, peer], dbuf.at[t, me], send_sem.at[10 + t], recv_sem.at[10 + t],
                    device_id={"tensor": peer}, device_id_type=MESH,
                ).start()

            return carry

        lax.fori_loop(0, n, step, 0)

    def total(t):
        drain(dbuf.at[t, others], recv_sem.at[10 + t])
        terms = [dbuf[t, z].astype(F32) for z in range(n)]
        while len(terms) > 1:
            terms = [a + b for a, b in zip(terms[::2], terms[1::2])]
        return terms[0].astype(BF16)

    gathered(0)
    project(0)

    @pl.when(seg > 0)
    def _():
        gathered(1)

    project(1)

    loads[3].wait()
    for p in range(16):
        for g in range(KVH):
            for part in range(2):
                if p < span:
                    col = (part * KVH + g) * HD
                    v = cache[0, p, :, col : col + HD].astype(F32)
                else:
                    v = jnp.zeros((ROWS2, HD), F32)
                kvt[part, pl.ds(g * 16 + p, ROWS2, stride=slots), :] = v
    for b in range(ROWS2):
        for part, dst in enumerate((kbuf, vbuf)):
            dst[b] = kvt[part, b * slots : (b + 1) * slots, :].astype(BF16)

    attend(0)
    attend(1)
    loads[6].wait()
    combine(0)
    combine(1)

    waiting[0] = total(0)

    @pl.when(not_last)
    def _():
        pass_on(waiting.at[0], waiting.at[1], 13).start()

    drain(state.at[0, others], send_sem.at[0])
    for t in range(2):
        drain(qbuf.at[t, others], send_sem.at[2 + t])
        owned = lax.rem(me, 4) == 2 * t

        @pl.when(owned)
        def _():
            drain(kvsrc.at[t, pl.ds(0, 3)], send_sem.at[4 + t])

        @pl.when(jnp.logical_not(owned))
        def _():
            drain(kvsrc.at[t], send_sem.at[4 + t])

        drain(obuf.at[t, others], send_sem.at[6 + t])
        drain(stbuf.at[t, others], send_sem.at[8 + t])
    drain(dbuf.at[0, others], send_sem.at[10])

    @pl.when(seg > 0)
    def _():
        drain(state.at[1, others], send_sem.at[1])

    res_ref[1] = unstack(total(1).astype(F32)).astype(BF16)

    @pl.when(seg > 0)
    def _():
        drain(waiting.at[1], recv_sem.at[13])

    res_ref[0] = unstack(state[1, me].astype(F32) + waiting[1].astype(F32)).astype(BF16)
    drain(dbuf.at[1, others], send_sem.at[11])

    @pl.when(not_last)
    def _():
        drain(ssrc_state.at[1], send_sem.at[12])
        drain(waiting.at[0], send_sem.at[13])


def solution(mesh):
    n = mesh.shape["tensor"]
    n_seg = mesh.shape["segment"]

    def local(h_init, y_init, norm_gain, w_query, w_kv, w_out, cache, lengths):
        hbm = pl.BlockSpec(memory_space=pltpu.HBM)
        vmem = pl.BlockSpec(memory_space=pltpu.VMEM)
        cache = jnp.transpose(cache, (0, 2, 1, 3))
        tile = (ROWS2, HD)
        both = pl.pallas_call(
            functools.partial(kernel, n, n_seg),
            out_shape=jax.ShapeDtypeStruct((2,) + h_init.shape, BF16),
            in_specs=[hbm] * 8,
            out_specs=vmem,
            scratch_shapes=[
                pltpu.VMEM(h_init.shape, BF16),
                pltpu.VMEM(y_init.shape, BF16),
                pltpu.VMEM(norm_gain.shape, BF16),
                pltpu.VMEM(w_query.shape, BF16),
                pltpu.VMEM(w_kv.shape, BF16),
                pltpu.VMEM(w_out.shape, BF16),
                pltpu.VMEM(cache.shape, BF16),
                pltpu.SMEM(lengths.shape, jnp.int32),
                pltpu.VMEM((2,) + tile, BF16),
                pltpu.VMEM((2, n) + tile, BF16),
                pltpu.VMEM((n, MB, 2 * HD), BF16),
                pltpu.VMEM(tile, F32),
                pltpu.VMEM(tile, F32),
                pltpu.VMEM((2,) + tile, BF16),
                pltpu.VMEM((2, n) + tile, BF16),
                pltpu.VMEM((MB * 2 * KVH, HD), F32),
                pltpu.VMEM((2, 4) + tile, BF16),
                pltpu.VMEM((2, n) + tile, BF16),
                pltpu.VMEM((2, ROWS2 * KVH * 16, HD), F32),
                pltpu.VMEM((ROWS2, KVH * 16, HD), BF16),
                pltpu.VMEM((ROWS2, KVH * 16, HD), BF16),
                pltpu.VMEM((MB * HEADS, HD), F32),
                pltpu.VMEM((MB * HEADS, HD), F32),
                pltpu.VMEM((2, n) + tile, BF16),
                pltpu.VMEM((2, n) + tile, BF16),
                pltpu.VMEM((2, n, 1, HD), F32),
                pltpu.VMEM((2, n, 1, HD), F32),
                pltpu.VMEM((2, n) + tile, BF16),
                pltpu.VMEM((2, n) + tile, BF16),
                pltpu.VMEM((2,) + tile, BF16),
                pltpu.SemaphoreType.DMA((8,)),
                pltpu.SemaphoreType.DMA((20,)),
                pltpu.SemaphoreType.DMA((20,)),
            ],
            compiler_params=pltpu.CompilerParams(
                collective_id=0, has_side_effects=True, vmem_limit_bytes=60 << 20
            ),
        )(h_init, y_init, norm_gain, w_query, w_kv, w_out, cache, lengths)
        return both[0], both[1]

    return jax.shard_map(
        local,
        mesh=mesh,
        in_specs=(
            P("segment", "tensor"),
            P("segment", "tensor"),
            P("segment", None),
            P("segment", None, "tensor"),
            P("segment", "tensor", None),
            P("segment", "tensor", None),
            P("segment", None, "tensor", None),
            P(),
        ),
        out_specs=(P("segment", "tensor"), P("segment", "tensor")),
        check_vma=False,
    )
```

```python
import functools
import math

import jax
import jax.numpy as jnp
from jax import lax
from jax.experimental import pallas as pl
from jax.experimental.pallas import tpu as pltpu
from jax.sharding import PartitionSpec as P

HEADS = 32
KVH = 4
HD = 128
TICKS = 2
MB = 8
ROWS2 = TICKS * MB
THETA = 500000.0
EPS = 1e-05
MASKED = -1e30
BIG = 1 << 30
MESH = pl.DeviceIdType.MESH
F32 = jnp.float32
BF16 = jnp.bfloat16


def far_first(i, me, n):
    d = n // 2 - (i + 1) // 2
    off = jnp.where(lax.rem(i, 2) == 1, d, n - d)
    return lax.rem(me + off, n)


def drain(ref, sem):
    pltpu.make_async_copy(ref, ref, sem).wait()


def stack_halves(v):
    return jnp.concatenate([v[:, :HD], v[:, HD:]], axis=0)


def unstack(v):
    return jnp.concatenate([v[:MB], v[MB:]], axis=1)


def kernel(
    n, n_seg, h_hbm, y_hbm, gain_hbm, wq_hbm, wkv_hbm, wo_hbm, cache_hbm, len_hbm,
    res_ref,
    h_in, y_in, gain, wq, wkv, wo, cache, len_ref,
    ssrc_state, state, nbuf, cosb, sinb,
    qsrc, qbuf, kvt32, kvsrc, kvbuf, kvt, kbuf, vbuf, qt, ot,
    osrc, obuf, stsrc, stbuf, dsrc, dbuf, waiting,
    load_sem, send_sem, recv_sem,
):
    me = lax.axis_index("tensor")
    seg = lax.axis_index("segment")
    first = seg == 0
    not_last = seg < n_seg - 1
    span = cache_hbm.shape[1]
    slots = KVH * 16
    others = pl.ds(0, n - 1)

    reach = n // 4
    near = [sign * d for d in range(reach, 0, -1) for sign in (1, -1)]

    def at(off):
        return lax.rem(me + (off + n), n)

    loads = [
        pltpu.make_async_copy(src, dst, load_sem.at[k])
        for k, (src, dst) in enumerate(
            [
                (h_hbm, h_in), (y_hbm, y_in), (gain_hbm, gain), (cache_hbm, cache),
                (wkv_hbm, wkv), (wq_hbm, wq), (wo_hbm, wo), (len_hbm, len_ref),
            ]
        )
    ]
    loads[0].start()
    loads[1].start()

    barrier = pltpu.get_barrier_semaphore()

    for off in near:
        pl.semaphore_signal(barrier, 1, device_id={"tensor": at(off)}, device_id_type=MESH)

    @pl.when(seg > 0)
    def _():
        pl.semaphore_signal(
            barrier, 1, device_id={"segment": seg - 1, "tensor": me}, device_id_type=MESH
        )

    for load in loads[2:]:
        load.start()
    loads[0].wait()
    loads[1].wait()

    def send_peers(*sends):
        def step(i, carry):
            peer = far_first(i, me, n)
            for src_of, dst, sems in sends:
                pltpu.make_async_remote_copy(
                    src_of(peer), dst, send_sem.at[sems], recv_sem.at[sems],
                    device_id={"tensor": peer}, device_id_type=MESH,
                ).start()
            return carry

        lax.fori_loop(0, n - 1, step, 0, unroll=True)

    def pass_on(src, dst, sems):
        return pltpu.make_async_remote_copy(
            src, dst, send_sem.at[sems], recv_sem.at[sems],
            device_id={"segment": seg + 1, "tensor": me}, device_id_type=MESH,
        )

    h32 = h_in[...].astype(F32)
    a32 = (h32 + y_in[...].astype(F32)).astype(BF16).astype(F32)
    h_block = stack_halves(h32).astype(BF16)
    ssrc_state[0] = h_block
    ssrc_state[1] = stack_halves(a32).astype(BF16)
    state[0, me] = h_block

    pl.semaphore_wait(barrier, jnp.where(not_last, 2 * reach + 1, 2 * reach))

    @pl.when(not_last)
    def _():
        pass_on(ssrc_state.at[1], state.at[1, me], 12).start()

    def spread(t, src):
        for off in near:
            sem = 14 + t if off == reach else 16 + t if off == -reach else t
            pltpu.make_async_remote_copy(
                src, state.at[t, me], send_sem.at[t], recv_sem.at[sem],
                device_id={"tensor": at(off)}, device_id_type=MESH,
            ).start()

    def relay(t):
        for sign, sem in ((1, 14 + t), (-1, 16 + t)):
            block = state.at[t, at(-sign * reach)]
            drain(block, recv_sem.at[sem])
            for d in range(reach if sign == 1 else reach - 1, 0, -1):
                pltpu.make_async_remote_copy(
                    block, block, send_sem.at[t], recv_sem.at[18 + t],
                    device_id={"tensor": at(sign * d)}, device_id_type=MESH,
                ).start()

    def gathered(t):
        drain(state.at[t, pl.ds(0, 2 * reach - 2)], recv_sem.at[t])
        drain(state.at[t, pl.ds(0, 2 * reach - 1)], recv_sem.at[18 + t])

    spread(0, ssrc_state.at[0])

    loads[7].wait()
    row16 = lax.broadcasted_iota(jnp.int32, (ROWS2, HD), 0)
    lane16 = lax.broadcasted_iota(jnp.int32, (ROWS2, HD), 1)
    base1 = jnp.maximum(seg - 1, 0) * MB
    seen = [len_ref[seg * MB + b] for b in range(MB)] + [
        jnp.where(first, 0, len_ref[base1 + b]) for b in range(MB)
    ]
    seen_rows = jnp.zeros((ROWS2, HD), jnp.int32)
    for b in range(ROWS2):
        seen_rows = jnp.where(row16 == b, seen[b], seen_rows)
    half_lane = jnp.where(lane16 < HD // 2, lane16, lane16 - HD // 2)
    freqs = jnp.exp(-math.log(THETA) * (2.0 * half_lane.astype(F32) / HD))
    angles = seen_rows.astype(F32) * freqs
    sines = jnp.sin(angles)
    cosb[...] = jnp.cos(angles)
    sinb[...] = jnp.where(lane16 < HD // 2, -sines, sines)
    @pl.when(seg > 0)
    def _():
        drain(ssrc_state.at[1], recv_sem.at[12])
        spread(1, state.at[1, me])

    relay(0)

    @pl.when(seg > 0)
    def _():
        relay(1)

    loads[2].wait()

    @pl.when(first)
    def _():
        state[1] = jnp.zeros_like(state[1])
        waiting[1] = jnp.zeros_like(waiting[1])

    loads[4].wait()
    loads[5].wait()
    jrow = lax.broadcasted_iota(jnp.int32, (HEADS, slots), 0)
    kcol = lax.broadcasted_iota(jnp.int32, (HEADS, slots), 1)
    same = lax.rem(jrow, 16) // 4 == kcol // 16
    slot = lax.rem(kcol, 16)
    place = jnp.where(same & (slot < span), me * span + slot, BIG)
    own_slot = same & (slot == span)
    lane32 = lax.broadcasted_iota(jnp.int32, (HEADS, HD), 1)
    krow = lax.broadcasted_iota(jnp.int32, (slots, HD), 0)
    scale = HD ** (-0.5)

    def project(t):
        chunks = []
        for z in range(n):
            v = state[t, z].astype(F32)
            chunks += [v[:MB], v[MB:]]
        squares = [c * c for c in chunks]
        while len(squares) > 1:
            squares = [a + b for a, b in zip(squares[::2], squares[1::2])]
        mean = jnp.sum(squares[0], axis=-1, keepdims=True) / (n * 2 * HD)
        inv = lax.rsqrt(mean + EPS)
        normed = []
        for k, c in enumerate(chunks):
            g = gain[0:1, k * HD : (k + 1) * HD].astype(F32)
            normed.append((c * inv * g).astype(BF16))
        for z in range(n):
            nbuf[z] = jnp.concatenate(normed[2 * z : 2 * z + 2], axis=1)
        kv = jnp.dot(nbuf[me], wkv[0], preferred_element_type=F32)
        for c in range(2 * KVH):
            kvt32[pl.ds(c, MB, stride=2 * KVH), :] = kv[:, c * HD : (c + 1) * HD]
        for o in range(4):
            kvsrc[t, o] = kvt32[o * 16 : (o + 1) * 16, :].astype(BF16)
        q32 = jnp.dot(jnp.concatenate(normed, axis=1), wq[0], preferred_element_type=F32)
        cosine = cosb[t * MB : (t + 1) * MB]
        sine = sinb[t * MB : (t + 1) * MB]
        turned = []
        for i in range(2):
            v = q32[:, i * HD : (i + 1) * HD]
            turned.append(v * cosine + pltpu.roll(v, HD // 2, 1) * sine)
        q = jnp.concatenate(turned, axis=0).astype(BF16)
        qsrc[t] = q
        qbuf[t, me] = q
        for o in range(4):
            owner = 4 * o + 2 * t

            @pl.when(me == owner)
            def _():
                kvbuf[t, owner] = kvsrc[t, o]

            @pl.when(me != owner)
            def _():
                pltpu.make_async_remote_copy(
                    kvsrc.at[t, o], kvbuf.at[t, me], send_sem.at[4 + t], recv_sem.at[4 + t],
                    device_id={"tensor": owner}, device_id_type=MESH,
                ).start()

        send_peers((lambda peer: qsrc.at[t], qbuf.at[t, me], 2 + t))

    def attend(t):
        @pl.when(lax.rem(me, 4) == 2 * t)
        def _():
            drain(kvbuf.at[t, others], recv_sem.at[4 + t])
            terms = [kvbuf[t, z].astype(F32) for z in range(n)]
            while len(terms) > 1:
                terms = [a + b for a, b in zip(terms[::2], terms[1::2])]
            fresh = terms[0]
            rolled = pltpu.roll(fresh, HD // 2, 1)
            for j in range(2):
                row = t * MB + (me // 4) * 2 + j
                at = j * 2 * KVH
                keys = (
                    fresh[at : at + KVH] * cosb[pl.ds(row, 1), :]
                    + rolled[at : at + KVH] * sinb[pl.ds(row, 1), :]
                )
                for dst, val in ((kbuf, keys), (vbuf, fresh[at + KVH : at + 2 * KVH])):
                    spread = jnp.concatenate(
                        [jnp.broadcast_to(val[g : g + 1], (16, HD)) for g in range(KVH)], axis=0
                    )
                    old = dst[row].astype(F32)
                    dst[row] = jnp.where(lax.rem(krow, 16) == span, spread, old).astype(BF16)

        drain(qbuf.at[t, others], recv_sem.at[2 + t])
        for r in range(n):
            v = qbuf[t, r].astype(F32)
            for i in range(2):
                qt[pl.ds(i * n + r, MB, stride=2 * n), :] = v[i * MB : (i + 1) * MB]
        scores = [
            lax.dot_general(
                qt[b * HEADS : (b + 1) * HEADS, :].astype(BF16),
                kbuf[t * MB + b],
                (((1,), (1,)), ((), ())),
                preferred_element_type=F32,
            )
            for b in range(MB)
        ]
        stats = jnp.zeros((HEADS, HD), F32)
        weights = []
        for b in range(MB):
            own_place = jnp.where(me == 4 * (b // 2) + 2 * t, -1, BIG)
            valid = jnp.where(own_slot, own_place, place) < seen[t * MB + b]
            s = jnp.where(valid, scores[b] * scale, MASKED)
            peak = jnp.max(s, axis=-1, keepdims=True)
            w = jnp.where(valid, jnp.exp(s - peak), 0.0)
            total = jnp.sum(w, axis=-1, keepdims=True)
            weights.append(w.astype(BF16))
            stats = jnp.where(lane32 == b, peak, stats)
            stats = jnp.where(lane32 == MB + b, total, stats)
        for b in range(MB):
            ot[b * HEADS : (b + 1) * HEADS, :] = jnp.dot(
                weights[b], vbuf[t * MB + b], preferred_element_type=F32
            )
        packed = jnp.where(lane32[:n] < 2 * MB, stats[:n], pltpu.roll(stats[n:], 2 * MB, 1))
        for r in range(n):
            stsrc[t, r] = packed[r : r + 1, :]
            osrc[t, r] = jnp.concatenate(
                [ot[pl.ds(i * n + r, MB, stride=2 * n), :] for i in range(2)], axis=0
            ).astype(BF16)
        obuf[t, me] = osrc[t, me]
        stbuf[t, me] = stsrc[t, me]
        send_peers(
            (lambda peer: stsrc.at[t, peer], stbuf.at[t, me], 8 + t),
            (lambda peer: osrc.at[t, peer], obuf.at[t, me], 6 + t),
        )

    def combine(t):
        drain(stbuf.at[t, others], recv_sem.at[8 + t])
        by_row = jnp.transpose(jnp.concatenate([stbuf[t, r] for r in range(n)], axis=0))
        shares = []
        for i in range(2):
            peaks = by_row[i * 16 : i * 16 + 8]
            totals = by_row[i * 16 + 8 : i * 16 + 16]
            scales = jnp.exp(peaks - jnp.max(peaks, axis=-1, keepdims=True))
            shares.append(scales / jnp.sum(scales * totals, axis=-1, keepdims=True))
        share = jnp.concatenate(shares, axis=0)
        drain(obuf.at[t, others], recv_sem.at[6 + t])
        terms = [obuf[t, r].astype(F32) * share[:, r : r + 1] for r in range(n)]
        while len(terms) > 1:
            terms = [a + b for a, b in zip(terms[::2], terms[1::2])]
        ctx = unstack(terms[0]).astype(BF16)
        out = jnp.dot(ctx, wo[0], preferred_element_type=F32)
        for c in range(n):
            dsrc[t, c] = stack_halves(out[:, c * 2 * HD : (c + 1) * 2 * HD]).astype(BF16)
        dbuf[t, me] = dsrc[t, me]
        def step(peer, carry):
            @pl.when(peer != me)
            def _():
                pltpu.make_async_remote_copy(
                    dsrc.at[t, peer], dbuf.at[t, me], send_sem.at[10 + t], recv_sem.at[10 + t],
                    device_id={"tensor": peer}, device_id_type=MESH,
                ).start()

            return carry

        lax.fori_loop(0, n, step, 0)

    def total(t):
        drain(dbuf.at[t, others], recv_sem.at[10 + t])
        terms = [dbuf[t, z].astype(F32) for z in range(n)]
        while len(terms) > 1:
            terms = [a + b for a, b in zip(terms[::2], terms[1::2])]
        return terms[0].astype(BF16)

    gathered(0)
    project(0)

    @pl.when(seg > 0)
    def _():
        gathered(1)

    project(1)

    loads[3].wait()
    for p in range(16):
        for g in range(KVH):
            for part in range(2):
                if p < span:
                    col = (part * KVH + g) * HD
                    v = cache[0, p, :, col : col + HD].astype(F32)
                else:
                    v = jnp.zeros((ROWS2, HD), F32)
                kvt[part, pl.ds(g * 16 + p, ROWS2, stride=slots), :] = v
    for b in range(ROWS2):
        for part, dst in enumerate((kbuf, vbuf)):
            dst[b] = kvt[part, b * slots : (b + 1) * slots, :].astype(BF16)

    attend(0)
    attend(1)
    loads[6].wait()
    combine(0)
    combine(1)

    waiting[0] = total(0)

    @pl.when(not_last)
    def _():
        pass_on(waiting.at[0], waiting.at[1], 13).start()

    drain(state.at[0, others], send_sem.at[0])
    for t in range(2):
        drain(qbuf.at[t, others], send_sem.at[2 + t])
        owned = lax.rem(me, 4) == 2 * t

        @pl.when(owned)
        def _():
            drain(kvsrc.at[t, pl.ds(0, 3)], send_sem.at[4 + t])

        @pl.when(jnp.logical_not(owned))
        def _():
            drain(kvsrc.at[t], send_sem.at[4 + t])

        drain(obuf.at[t, others], send_sem.at[6 + t])
        drain(stbuf.at[t, others], send_sem.at[8 + t])
    drain(dbuf.at[0, others], send_sem.at[10])

    @pl.when(seg > 0)
    def _():
        drain(state.at[1, others], send_sem.at[1])

    res_ref[1] = unstack(total(1).astype(F32)).astype(BF16)

    @pl.when(seg > 0)
    def _():
        drain(waiting.at[1], recv_sem.at[13])

    res_ref[0] = unstack(state[1, me].astype(F32) + waiting[1].astype(F32)).astype(BF16)
    drain(dbuf.at[1, others], send_sem.at[11])

    @pl.when(not_last)
    def _():
        drain(ssrc_state.at[1], send_sem.at[12])
        drain(waiting.at[0], send_sem.at[13])


def solution(mesh):
    n = mesh.shape["tensor"]
    n_seg = mesh.shape["segment"]

    def local(h_init, y_init, norm_gain, w_query, w_kv, w_out, cache, lengths):
        hbm = pl.BlockSpec(memory_space=pltpu.HBM)
        vmem = pl.BlockSpec(memory_space=pltpu.VMEM)
        cache = jnp.transpose(cache, (0, 2, 1, 3))
        tile = (ROWS2, HD)
        both = pl.pallas_call(
            functools.partial(kernel, n, n_seg),
            out_shape=jax.ShapeDtypeStruct((2,) + h_init.shape, BF16),
            in_specs=[hbm] * 8,
            out_specs=vmem,
            scratch_shapes=[
                pltpu.VMEM(h_init.shape, BF16),
                pltpu.VMEM(y_init.shape, BF16),
                pltpu.VMEM(norm_gain.shape, BF16),
                pltpu.VMEM(w_query.shape, BF16),
                pltpu.VMEM(w_kv.shape, BF16),
                pltpu.VMEM(w_out.shape, BF16),
                pltpu.VMEM(cache.shape, BF16),
                pltpu.SMEM(lengths.shape, jnp.int32),
                pltpu.VMEM((2,) + tile, BF16),
                pltpu.VMEM((2, n) + tile, BF16),
                pltpu.VMEM((n, MB, 2 * HD), BF16),
                pltpu.VMEM(tile, F32),
                pltpu.VMEM(tile, F32),
                pltpu.VMEM((2,) + tile, BF16),
                pltpu.VMEM((2, n) + tile, BF16),
                pltpu.VMEM((MB * 2 * KVH, HD), F32),
                pltpu.VMEM((2, 4) + tile, BF16),
                pltpu.VMEM((2, n) + tile, BF16),
                pltpu.VMEM((2, ROWS2 * KVH * 16, HD), F32),
                pltpu.VMEM((ROWS2, KVH * 16, HD), BF16),
                pltpu.VMEM((ROWS2, KVH * 16, HD), BF16),
                pltpu.VMEM((MB * HEADS, HD), F32),
                pltpu.VMEM((MB * HEADS, HD), F32),
                pltpu.VMEM((2, n) + tile, BF16),
                pltpu.VMEM((2, n) + tile, BF16),
                pltpu.VMEM((2, n, 1, HD), F32),
                pltpu.VMEM((2, n, 1, HD), F32),
                pltpu.VMEM((2, n) + tile, BF16),
                pltpu.VMEM((2, n) + tile, BF16),
                pltpu.VMEM((2,) + tile, BF16),
                pltpu.SemaphoreType.DMA((8,)),
                pltpu.SemaphoreType.DMA((20,)),
                pltpu.SemaphoreType.DMA((20,)),
            ],
            compiler_params=pltpu.CompilerParams(
                collective_id=0, has_side_effects=True, vmem_limit_bytes=60 << 20
            ),
        )(h_init, y_init, norm_gain, w_query, w_kv, w_out, cache, lengths)
        return both[0], both[1]

    return jax.shard_map(
        local,
        mesh=mesh,
        in_specs=(
            P("segment", "tensor"),
            P("segment", "tensor"),
            P("segment", None),
            P("segment", None, "tensor"),
            P("segment", "tensor", None),
            P("segment", "tensor", None),
            P("segment", None, "tensor", None),
            P(),
        ),
        out_specs=(P("segment", "tensor"), P("segment", "tensor")),
        check_vma=False,
    )
```

```python
import functools
import math

import jax
import jax.numpy as jnp
from jax import lax
from jax.experimental import pallas as pl
from jax.experimental.pallas import tpu as pltpu
from jax.sharding import PartitionSpec as P

HEADS = 32
KVH = 4
HD = 128
TICKS = 2
MB = 8
ROWS2 = TICKS * MB
THETA = 500000.0
EPS = 1e-05
MASKED = -1e30
BIG = 1 << 30
MESH = pl.DeviceIdType.MESH
F32 = jnp.float32
BF16 = jnp.bfloat16


def far_first(i, me, n):
    d = n // 2 - (i + 1) // 2
    off = jnp.where(lax.rem(i, 2) == 1, d, n - d)
    return lax.rem(me + off, n)


def drain(ref, sem):
    pltpu.make_async_copy(ref, ref, sem).wait()


def stack_halves(v):
    return jnp.concatenate([v[:, :HD], v[:, HD:]], axis=0)


def unstack(v):
    return jnp.concatenate([v[:MB], v[MB:]], axis=1)


def kernel(
    n, n_seg, h_hbm, y_hbm, gain_hbm, wq_hbm, wkv_hbm, wo_hbm, cache_hbm, len_hbm,
    res_ref,
    h_in, y_in, gain, wq, wkv, wo, cache, len_ref,
    ssrc_state, state, nbuf, cosb, sinb,
    qsrc, qbuf, kvt32, kvsrc, kvbuf, kvt, kbuf, vbuf, qt, ot,
    osrc, obuf, stsrc, stbuf, dsrc, dbuf, waiting,
    load_sem, send_sem, recv_sem,
):
    me = lax.axis_index("tensor")
    seg = lax.axis_index("segment")
    first = seg == 0
    not_last = seg < n_seg - 1
    span = cache_hbm.shape[1]
    slots = KVH * 16
    others = pl.ds(0, n - 1)

    reach = n // 4
    near = [sign * d for d in range(reach, 0, -1) for sign in (1, -1)]

    def at(off):
        return lax.rem(me + (off + n), n)

    loads = [
        pltpu.make_async_copy(src, dst, load_sem.at[k])
        for k, (src, dst) in enumerate(
            [
                (h_hbm, h_in), (y_hbm, y_in), (gain_hbm, gain), (cache_hbm, cache),
                (wkv_hbm, wkv), (wq_hbm, wq), (wo_hbm, wo), (len_hbm, len_ref),
            ]
        )
    ]
    loads[0].start()
    loads[1].start()

    barrier = pltpu.get_barrier_semaphore()

    for off in near:
        pl.semaphore_signal(barrier, 1, device_id={"tensor": at(off)}, device_id_type=MESH)

    @pl.when(seg > 0)
    def _():
        pl.semaphore_signal(
            barrier, 1, device_id={"segment": seg - 1, "tensor": me}, device_id_type=MESH
        )

    for load in loads[2:]:
        load.start()
    loads[0].wait()
    loads[1].wait()

    def send_peers(*sends):
        def step(i, carry):
            peer = far_first(i, me, n)
            for src_of, dst, sems in sends:
                pltpu.make_async_remote_copy(
                    src_of(peer), dst, send_sem.at[sems], recv_sem.at[sems],
                    device_id={"tensor": peer}, device_id_type=MESH,
                ).start()
            return carry

        lax.fori_loop(0, n - 1, step, 0, unroll=True)

    def pass_on(src, dst, sems):
        return pltpu.make_async_remote_copy(
            src, dst, send_sem.at[sems], recv_sem.at[sems],
            device_id={"segment": seg + 1, "tensor": me}, device_id_type=MESH,
        )

    h32 = h_in[...].astype(F32)
    a32 = (h32 + y_in[...].astype(F32)).astype(BF16).astype(F32)
    h_block = stack_halves(h32).astype(BF16)
    ssrc_state[0] = h_block
    ssrc_state[1] = stack_halves(a32).astype(BF16)
    state[0, me] = h_block

    pl.semaphore_wait(barrier, jnp.where(not_last, 2 * reach + 1, 2 * reach))

    @pl.when(not_last)
    def _():
        pass_on(ssrc_state.at[1], state.at[1, me], 12).start()

    def spread(t, src):
        for off in near:
            sem = 14 + t if off == reach else 16 + t if off == -reach else t
            pltpu.make_async_remote_copy(
                src, state.at[t, me], send_sem.at[t], recv_sem.at[sem],
                device_id={"tensor": at(off)}, device_id_type=MESH,
            ).start()

    def relay(t):
        for sign, sem in ((1, 14 + t), (-1, 16 + t)):
            block = state.at[t, at(-sign * reach)]
            drain(block, recv_sem.at[sem])
            for d in range(reach if sign == 1 else reach - 1, 0, -1):
                pltpu.make_async_remote_copy(
                    block, block, send_sem.at[t], recv_sem.at[18 + t],
                    device_id={"tensor": at(sign * d)}, device_id_type=MESH,
                ).start()

    def gathered(t):
        drain(state.at[t, pl.ds(0, 2 * reach - 2)], recv_sem.at[t])
        drain(state.at[t, pl.ds(0, 2 * reach - 1)], recv_sem.at[18 + t])

    spread(0, ssrc_state.at[0])

    loads[7].wait()
    row16 = lax.broadcasted_iota(jnp.int32, (ROWS2, HD), 0)
    lane16 = lax.broadcasted_iota(jnp.int32, (ROWS2, HD), 1)
    base1 = jnp.maximum(seg - 1, 0) * MB
    seen = [len_ref[seg * MB + b] for b in range(MB)] + [
        jnp.where(first, 0, len_ref[base1 + b]) for b in range(MB)
    ]
    seen_rows = jnp.zeros((ROWS2, HD), jnp.int32)
    for b in range(ROWS2):
        seen_rows = jnp.where(row16 == b, seen[b], seen_rows)
    half_lane = jnp.where(lane16 < HD // 2, lane16, lane16 - HD // 2)
    freqs = jnp.exp(-math.log(THETA) * (2.0 * half_lane.astype(F32) / HD))
    angles = seen_rows.astype(F32) * freqs
    sines = jnp.sin(angles)
    cosb[...] = jnp.cos(angles)
    sinb[...] = jnp.where(lane16 < HD // 2, -sines, sines)
    @pl.when(seg > 0)
    def _():
        drain(ssrc_state.at[1], recv_sem.at[12])
        spread(1, state.at[1, me])

    relay(0)

    @pl.when(seg > 0)
    def _():
        relay(1)

    loads[2].wait()

    @pl.when(first)
    def _():
        state[1] = jnp.zeros_like(state[1])
        waiting[1] = jnp.zeros_like(waiting[1])

    loads[4].wait()
    loads[5].wait()
    jrow = lax.broadcasted_iota(jnp.int32, (HEADS, slots), 0)
    kcol = lax.broadcasted_iota(jnp.int32, (HEADS, slots), 1)
    same = lax.rem(jrow, 16) // 4 == kcol // 16
    slot = lax.rem(kcol, 16)
    place = jnp.where(same & (slot < span), me * span + slot, BIG)
    own_slot = same & (slot == span)
    lane32 = lax.broadcasted_iota(jnp.int32, (HEADS, HD), 1)
    krow = lax.broadcasted_iota(jnp.int32, (slots, HD), 0)
    scale = HD ** (-0.5)

    def project(t):
        chunks = []
        for z in range(n):
            v = state[t, z].astype(F32)
            chunks += [v[:MB], v[MB:]]
        squares = [c * c for c in chunks]
        while len(squares) > 1:
            squares = [a + b for a, b in zip(squares[::2], squares[1::2])]
        mean = jnp.sum(squares[0], axis=-1, keepdims=True) / (n * 2 * HD)
        inv = lax.rsqrt(mean + EPS)
        normed = []
        for k, c in enumerate(chunks):
            g = gain[0:1, k * HD : (k + 1) * HD].astype(F32)
            normed.append((c * inv * g).astype(BF16))
        for z in range(n):
            nbuf[z] = jnp.concatenate(normed[2 * z : 2 * z + 2], axis=1)
        kv = jnp.dot(nbuf[me], wkv[0], preferred_element_type=F32)
        for c in range(2 * KVH):
            kvt32[pl.ds(c, MB, stride=2 * KVH), :] = kv[:, c * HD : (c + 1) * HD]
        for o in range(4):
            kvsrc[t, o] = kvt32[o * 16 : (o + 1) * 16, :].astype(BF16)
        q32 = jnp.dot(jnp.concatenate(normed, axis=1), wq[0], preferred_element_type=F32)
        cosine = cosb[t * MB : (t + 1) * MB]
        sine = sinb[t * MB : (t + 1) * MB]
        turned = []
        for i in range(2):
            v = q32[:, i * HD : (i + 1) * HD]
            turned.append(v * cosine + pltpu.roll(v, HD // 2, 1) * sine)
        q = jnp.concatenate(turned, axis=0).astype(BF16)
        qsrc[t] = q
        qbuf[t, me] = q
        for k in (2, 1, 3, 0):
            o = lax.rem(me // 4 + k, 4)
            owner = 4 * o + 2 * t

            @pl.when(me == owner)
            def _():
                kvbuf[t, owner] = kvsrc[t, o]

            @pl.when(me != owner)
            def _():
                pltpu.make_async_remote_copy(
                    kvsrc.at[t, o], kvbuf.at[t, me], send_sem.at[4 + t], recv_sem.at[4 + t],
                    device_id={"tensor": owner}, device_id_type=MESH,
                ).start()

        send_peers((lambda peer: qsrc.at[t], qbuf.at[t, me], 2 + t))

    def attend(t):
        @pl.when(lax.rem(me, 4) == 2 * t)
        def _():
            drain(kvbuf.at[t, others], recv_sem.at[4 + t])
            terms = [kvbuf[t, z].astype(F32) for z in range(n)]
            while len(terms) > 1:
                terms = [a + b for a, b in zip(terms[::2], terms[1::2])]
            fresh = terms[0]
            rolled = pltpu.roll(fresh, HD // 2, 1)
            for j in range(2):
                row = t * MB + (me // 4) * 2 + j
                at = j * 2 * KVH
                keys = (
                    fresh[at : at + KVH] * cosb[pl.ds(row, 1), :]
                    + rolled[at : at + KVH] * sinb[pl.ds(row, 1), :]
                )
                for dst, val in ((kbuf, keys), (vbuf, fresh[at + KVH : at + 2 * KVH])):
                    spread = jnp.concatenate(
                        [jnp.broadcast_to(val[g : g + 1], (16, HD)) for g in range(KVH)], axis=0
                    )
                    old = dst[row].astype(F32)
                    dst[row] = jnp.where(lax.rem(krow, 16) == span, spread, old).astype(BF16)

        drain(qbuf.at[t, others], recv_sem.at[2 + t])
        for r in range(n):
            v = qbuf[t, r].astype(F32)
            for i in range(2):
                qt[pl.ds(i * n + r, MB, stride=2 * n), :] = v[i * MB : (i + 1) * MB]
        scores = [
            lax.dot_general(
                qt[b * HEADS : (b + 1) * HEADS, :].astype(BF16),
                kbuf[t * MB + b],
                (((1,), (1,)), ((), ())),
                preferred_element_type=F32,
            )
            for b in range(MB)
        ]
        stats = jnp.zeros((HEADS, HD), F32)
        weights = []
        for b in range(MB):
            own_place = jnp.where(me == 4 * (b // 2) + 2 * t, -1, BIG)
            valid = jnp.where(own_slot, own_place, place) < seen[t * MB + b]
            s = jnp.where(valid, scores[b] * scale, MASKED)
            peak = jnp.max(s, axis=-1, keepdims=True)
            w = jnp.where(valid, jnp.exp(s - peak), 0.0)
            total = jnp.sum(w, axis=-1, keepdims=True)
            weights.append(w.astype(BF16))
            stats = jnp.where(lane32 == b, peak, stats)
            stats = jnp.where(lane32 == MB + b, total, stats)
        for b in range(MB):
            ot[b * HEADS : (b + 1) * HEADS, :] = jnp.dot(
                weights[b], vbuf[t * MB + b], preferred_element_type=F32
            )
        packed = jnp.where(lane32[:n] < 2 * MB, stats[:n], pltpu.roll(stats[n:], 2 * MB, 1))
        for r in range(n):
            stsrc[t, r] = packed[r : r + 1, :]
            osrc[t, r] = jnp.concatenate(
                [ot[pl.ds(i * n + r, MB, stride=2 * n), :] for i in range(2)], axis=0
            ).astype(BF16)
        obuf[t, me] = osrc[t, me]
        stbuf[t, me] = stsrc[t, me]
        send_peers(
            (lambda peer: osrc.at[t, peer], obuf.at[t, me], 6 + t),
            (lambda peer: stsrc.at[t, peer], stbuf.at[t, me], 8 + t),
        )

    def combine(t):
        drain(stbuf.at[t, others], recv_sem.at[8 + t])
        by_row = jnp.transpose(jnp.concatenate([stbuf[t, r] for r in range(n)], axis=0))
        shares = []
        for i in range(2):
            peaks = by_row[i * 16 : i * 16 + 8]
            totals = by_row[i * 16 + 8 : i * 16 + 16]
            scales = jnp.exp(peaks - jnp.max(peaks, axis=-1, keepdims=True))
            shares.append(scales / jnp.sum(scales * totals, axis=-1, keepdims=True))
        share = jnp.concatenate(shares, axis=0)
        drain(obuf.at[t, others], recv_sem.at[6 + t])
        terms = [obuf[t, r].astype(F32) * share[:, r : r + 1] for r in range(n)]
        while len(terms) > 1:
            terms = [a + b for a, b in zip(terms[::2], terms[1::2])]
        ctx = unstack(terms[0]).astype(BF16)
        out = jnp.dot(ctx, wo[0], preferred_element_type=F32)
        for c in range(n):
            dsrc[t, c] = stack_halves(out[:, c * 2 * HD : (c + 1) * 2 * HD]).astype(BF16)
        dbuf[t, me] = dsrc[t, me]
        def step(peer, carry):
            @pl.when(peer != me)
            def _():
                pltpu.make_async_remote_copy(
                    dsrc.at[t, peer], dbuf.at[t, me], send_sem.at[10 + t], recv_sem.at[10 + t],
                    device_id={"tensor": peer}, device_id_type=MESH,
                ).start()

            return carry

        lax.fori_loop(0, n, step, 0)

    def total(t):
        drain(dbuf.at[t, others], recv_sem.at[10 + t])
        terms = [dbuf[t, z].astype(F32) for z in range(n)]
        while len(terms) > 1:
            terms = [a + b for a, b in zip(terms[::2], terms[1::2])]
        return terms[0].astype(BF16)

    gathered(0)
    project(0)

    @pl.when(seg > 0)
    def _():
        gathered(1)

    project(1)

    loads[3].wait()
    for p in range(16):
        for g in range(KVH):
            for part in range(2):
                if p < span:
                    col = (part * KVH + g) * HD
                    v = cache[0, p, :, col : col + HD].astype(F32)
                else:
                    v = jnp.zeros((ROWS2, HD), F32)
                kvt[part, pl.ds(g * 16 + p, ROWS2, stride=slots), :] = v
    for b in range(ROWS2):
        for part, dst in enumerate((kbuf, vbuf)):
            dst[b] = kvt[part, b * slots : (b + 1) * slots, :].astype(BF16)

    attend(0)
    attend(1)
    loads[6].wait()
    combine(0)
    combine(1)

    waiting[0] = total(0)

    @pl.when(not_last)
    def _():
        pass_on(waiting.at[0], waiting.at[1], 13).start()

    drain(state.at[0, others], send_sem.at[0])
    for t in range(2):
        drain(qbuf.at[t, others], send_sem.at[2 + t])
        owned = lax.rem(me, 4) == 2 * t

        @pl.when(owned)
        def _():
            drain(kvsrc.at[t, pl.ds(0, 3)], send_sem.at[4 + t])

        @pl.when(jnp.logical_not(owned))
        def _():
            drain(kvsrc.at[t], send_sem.at[4 + t])

        drain(obuf.at[t, others], send_sem.at[6 + t])
        drain(stbuf.at[t, others], send_sem.at[8 + t])
    drain(dbuf.at[0, others], send_sem.at[10])

    @pl.when(seg > 0)
    def _():
        drain(state.at[1, others], send_sem.at[1])

    res_ref[1] = unstack(total(1).astype(F32)).astype(BF16)

    @pl.when(seg > 0)
    def _():
        drain(waiting.at[1], recv_sem.at[13])

    res_ref[0] = unstack(state[1, me].astype(F32) + waiting[1].astype(F32)).astype(BF16)
    drain(dbuf.at[1, others], send_sem.at[11])

    @pl.when(not_last)
    def _():
        drain(ssrc_state.at[1], send_sem.at[12])
        drain(waiting.at[0], send_sem.at[13])


def solution(mesh):
    n = mesh.shape["tensor"]
    n_seg = mesh.shape["segment"]

    def local(h_init, y_init, norm_gain, w_query, w_kv, w_out, cache, lengths):
        hbm = pl.BlockSpec(memory_space=pltpu.HBM)
        vmem = pl.BlockSpec(memory_space=pltpu.VMEM)
        cache = jnp.transpose(cache, (0, 2, 1, 3))
        tile = (ROWS2, HD)
        both = pl.pallas_call(
            functools.partial(kernel, n, n_seg),
            out_shape=jax.ShapeDtypeStruct((2,) + h_init.shape, BF16),
            in_specs=[hbm] * 8,
            out_specs=vmem,
            scratch_shapes=[
                pltpu.VMEM(h_init.shape, BF16),
                pltpu.VMEM(y_init.shape, BF16),
                pltpu.VMEM(norm_gain.shape, BF16),
                pltpu.VMEM(w_query.shape, BF16),
                pltpu.VMEM(w_kv.shape, BF16),
                pltpu.VMEM(w_out.shape, BF16),
                pltpu.VMEM(cache.shape, BF16),
                pltpu.SMEM(lengths.shape, jnp.int32),
                pltpu.VMEM((2,) + tile, BF16),
                pltpu.VMEM((2, n) + tile, BF16),
                pltpu.VMEM((n, MB, 2 * HD), BF16),
                pltpu.VMEM(tile, F32),
                pltpu.VMEM(tile, F32),
                pltpu.VMEM((2,) + tile, BF16),
                pltpu.VMEM((2, n) + tile, BF16),
                pltpu.VMEM((MB * 2 * KVH, HD), F32),
                pltpu.VMEM((2, 4) + tile, BF16),
                pltpu.VMEM((2, n) + tile, BF16),
                pltpu.VMEM((2, ROWS2 * KVH * 16, HD), F32),
                pltpu.VMEM((ROWS2, KVH * 16, HD), BF16),
                pltpu.VMEM((ROWS2, KVH * 16, HD), BF16),
                pltpu.VMEM((MB * HEADS, HD), F32),
                pltpu.VMEM((MB * HEADS, HD), F32),
                pltpu.VMEM((2, n) + tile, BF16),
                pltpu.VMEM((2, n) + tile, BF16),
                pltpu.VMEM((2, n, 1, HD), F32),
                pltpu.VMEM((2, n, 1, HD), F32),
                pltpu.VMEM((2, n) + tile, BF16),
                pltpu.VMEM((2, n) + tile, BF16),
                pltpu.VMEM((2,) + tile, BF16),
                pltpu.SemaphoreType.DMA((8,)),
                pltpu.SemaphoreType.DMA((20,)),
                pltpu.SemaphoreType.DMA((20,)),
            ],
            compiler_params=pltpu.CompilerParams(
                collective_id=0, has_side_effects=True, vmem_limit_bytes=60 << 20
            ),
        )(h_init, y_init, norm_gain, w_query, w_kv, w_out, cache, lengths)
        return both[0], both[1]

    return jax.shard_map(
        local,
        mesh=mesh,
        in_specs=(
            P("segment", "tensor"),
            P("segment", "tensor"),
            P("segment", None),
            P("segment", None, "tensor"),
            P("segment", "tensor", None),
            P("segment", "tensor", None),
            P("segment", None, "tensor", None),
            P(),
        ),
        out_specs=(P("segment", "tensor"), P("segment", "tensor")),
        check_vma=False,
    )
```
